256 devices in a mesh: pos: 16 (over x, z_lo), tile: 16 (over y, z_hi, core).
Axes of the slice: x: 4, y: 4, z: 8 (z_hi: 2, z_lo: 4; z = z_hi * 4 + z_lo), core: 2. Of those that a mesh axis runs over, the one named last changes fastest.
Arguments:
- object_slices: bfloat16 [16, 2, 2, 128, 1024], P('tile', None, None, 'pos'), may hold values from -4 to 4
- probe_modes: float32 [8, 2, 128, 128], replicated, may hold values from -4 to 4
- offsets: int32 [16, 16, 4, 2], P('tile', 'pos'), may hold values from 0 to 896, as said below
- counts: int32 [16, 16], P('tile', 'pos'), may hold values from 1 to 4, 32 in all within a row
- patterns: float32 [16, 16, 4, 128, 128], P('tile', 'pos'), may hold values from 0.05 to 36
Outputs:
- object_grad: float32 [16, 2, 2, 128, 1024], P('tile', None, None, 'pos')
- probe_grad: float32 [8, 2, 128, 128], replicated
The draws below stay inside these ranges and needn't reach their ends.
Inputs may be any that keep to these rules, and one draw needn't show every extreme that they name: `offsets`: entry 0 is a slot's row offset within its region's tile, and 0 in the last tile; entry 1 its column offset; so every footprint lies inside the object and reaches at most into the next tile. A device's live slots are its first counts slots; the counts of every region add up to 32.
All inputs are finite; a program needn't handle non-finite values.
Results may differ from the reference program's by a relative error of at most 0.0003.
Values may be sent and summed in bfloat16 or wider, within the bound.
A program may use at most 64 MiB of HBM per device.

```python
import math
import jax
import jax.numpy as jnp
import numpy as np
from jax import lax

PATCH = 128
MODES = 8
SLICES = 2
SLOTS = 4
OW = 1024
REGIONS = 16
PEERS = 16


def draw_offsets(key, part):
    key = jax.random.fold_in(key, 11)
    row_key, col_key = jax.random.split(key)
    shape = (REGIONS, PEERS, SLOTS)
    rows = jax.random.randint(row_key, shape, 0, PATCH)
    cols = jax.random.randint(col_key, shape, 0, OW - PATCH + 1)
    tile_rank = lax.broadcasted_iota(jnp.int32, shape, 0)
    peer_rank = lax.broadcasted_iota(jnp.int32, shape, 1)
    slot_rank = lax.broadcasted_iota(jnp.int32, shape, 2)
    rows = jnp.where(tile_rank == REGIONS - 1, 0, rows)
    first = (tile_rank == 0) & (peer_rank == 0) & (slot_rank == 0)
    rows = jnp.where(first, PATCH - 1, rows)
    cols = jnp.where(first, OW - PATCH, cols)
    return jnp.stack([rows, cols], axis=-1).astype(jnp.int32)


def device_factor(spread):
    shape = (REGIONS, PEERS, 1, 1, 1)
    tile_rank = lax.broadcasted_iota(jnp.int32, shape, 0)
    peer_rank = lax.broadcasted_iota(jnp.int32, shape, 1)
    flat = (tile_rank * PEERS + peer_rank).astype(jnp.float32)
    return jnp.exp(jnp.log(spread) * flat / (REGIONS * PEERS - 1))


def draw_patterns(key, part):
    key = jax.random.fold_in(key, 23)
    shape = (REGIONS, PEERS, SLOTS, PATCH, PATCH)
    expo = jax.random.uniform(key, shape, jnp.float32, jnp.log(0.05), jnp.log(4.0))
    return (jnp.exp(expo) * device_factor(3.0)).astype(jnp.float32)


def steps_of(key, extent, cuts, low, top_value):
    level = 1.0
    for position, blocks in cuts:
        heights = jax.random.uniform(jax.random.fold_in(jax.random.fold_in(key, 6), position), (blocks,), jnp.float32, low / len(cuts), top_value / len(cuts))
        level = level * jnp.repeat(jnp.exp(heights), extent[position] // blocks).reshape((-1,) + (1,) * (len(extent) - 1 - position))
    return level


def split_up(amount, total, most, lean):
    portions = [(1 << 20) // math.isqrt(grade ** lean) + 1 for grade in range(2, amount + 1)]
    surplus, given = total - most - (amount - 1), [1] * (amount - 1)
    while surplus > 0:
        free = [i for i in range(amount - 1) if given[i] < most]
        whole, left = sum([portions[i] for i in free]), surplus
        for i in free:
            extra = min(most - given[i], max(1, left * portions[i] // whole), surplus)
            given[i] = given[i] + extra
            surplus = surplus - extra
    return np.array([most] + given)


def uneven_parts(rng, amount, total, limit, slope):
    if amount == 2:
        one = jax.random.randint(rng, (), max(1, total - limit), min(limit, total - 1) + 1)
        return jnp.stack([one, total - one])
    tallies = jnp.asarray(split_up(amount, total, limit, slope), jnp.int32)
    twos = (amount - 1) // 2
    giver, sink = tallies[1:1 + 2 * twos:2], tallies[2:2 + 2 * twos:2]
    room = jnp.minimum(giver - 1, limit - sink)
    passed = jax.random.randint(jax.random.fold_in(rng, 1), (twos,), 0, 1 << 20) % (room + 1)
    tallies = tallies.at[1:1 + 2 * twos:2].set(giver - passed).at[2:2 + 2 * twos:2].set(sink + passed)
    return tallies[jax.random.permutation(jax.random.fold_in(rng, 2), amount)]


def scatter_about(rng, shape, scale, limit, shards=(), kind=jnp.bfloat16):
    gain = steps_of(rng, shape, shards, -0.22, 0.18) if shards else 1.0
    result = jax.random.normal(rng, shape, jnp.float32) * scale * gain
    return jnp.minimum(jnp.maximum(result, -limit), limit).astype(kind)


def setup_inputs(seed: int = 0) -> dict:
    arg_keys = jax.random.split(jax.random.key(seed), 6)
    return {
        "object_slices": scatter_about(arg_keys[0], (REGIONS, SLICES, 2, PATCH, OW), 0.7, 4.0, ((0, 16), (3, 16))),
        "probe_modes": scatter_about(arg_keys[1], (MODES, 2, PATCH, PATCH), ((2 * MODES) ** -0.5), 4.0, (), jnp.float32),
        "offsets": draw_offsets(jax.random.fold_in(arg_keys[5], 71), 0),
        "counts": jax.vmap(lambda own: uneven_parts(own, PEERS, SLOTS * PEERS // 2, SLOTS, 2))(jax.random.split(arg_keys[3], REGIONS)).reshape((REGIONS, PEERS)).astype(jnp.int32),
        "patterns": draw_patterns(jax.random.fold_in(arg_keys[5], 71), 0),
    }


fresnel_coef = 24.0

def fresnel_kernel(length, float_type):
    indices = jnp.arange(length, dtype=jnp.int32)
    frequency = ((indices + length // 2) % length - length // 2).astype(float_type) / length
    phase = -jnp.pi * fresnel_coef * (frequency[:, None] ** 2 + frequency[None, :] ** 2)
    return jnp.cos(phase) + 1j * jnp.sin(phase)

def position_loss(probe_modes, window, measured, kernel):
    wavefield = (probe_modes[:, 0] + 1j * probe_modes[:, 1]) * (window[0, 0] + 1j * window[0, 1])
    for slice_index in range(1, SLICES):
        spectrum = jnp.fft.fft2(wavefield, norm='ortho') * kernel
        wavefield = jnp.fft.ifft2(spectrum, norm='ortho') * (window[slice_index, 0] + 1j * window[slice_index, 1])
    far_field = jnp.fft.fft2(wavefield, norm='ortho')
    intensity = lax.optimization_barrier(jnp.sum(jnp.real(far_field) ** 2 + jnp.imag(far_field) ** 2, axis=0))
    return 0.5 * jnp.sum((intensity - measured) ** 2)

def reference(object_slices, probe_modes, offsets, counts, patterns):
    float_type = probe_modes.dtype
    object_full = jnp.transpose(object_slices.astype(jnp.float32), (1, 2, 0, 3, 4)).reshape(SLICES, 2, REGIONS * PATCH, OW)
    kernel = fresnel_kernel(PATCH, float_type)
    slot_total = REGIONS * PEERS * SLOTS
    flat_index = jnp.arange(slot_total, dtype=jnp.int32)
    region_index = flat_index // (PEERS * SLOTS)
    slot_index = flat_index % SLOTS
    live_mask = (slot_index < jnp.repeat(counts.reshape(-1), SLOTS)).astype(float_type)
    row_start = (region_index * PATCH + offsets[..., 0].reshape(-1)).astype(jnp.int32)
    col_start = offsets[..., 1].reshape(-1).astype(jnp.int32)
    measured_all = patterns.reshape(slot_total, PATCH, PATCH)
    zero_index = jnp.zeros((), jnp.int32)

    def accumulate(carry, inputs):
        object_grad, probe_grad = carry
        row_one, col_one, live_one, measured_one = inputs
        starts = (zero_index, zero_index, row_one, col_one)
        window = lax.dynamic_slice(object_full, starts, (SLICES, 2, PATCH, PATCH))

        def loss_of(probe_arg, window_arg):
            return live_one * position_loss(probe_arg, window_arg, measured_one, kernel)
        loss_value, pullback = jax.vjp(loss_of, probe_modes, window)
        probe_term, window_term = pullback(jnp.ones_like(loss_value))
        current = lax.dynamic_slice(object_grad, starts, (SLICES, 2, PATCH, PATCH))
        object_grad = lax.dynamic_update_slice(object_grad, current + window_term, starts)
        return ((object_grad, probe_grad + probe_term), loss_value)
    initial = (jnp.zeros_like(object_full), jnp.zeros_like(probe_modes))
    (object_grad, probe_grad), losses = lax.scan(accumulate, initial, (row_start, col_start, live_mask, measured_all))
    object_grad = jnp.transpose(object_grad.reshape(SLICES, 2, REGIONS, PATCH, OW), (2, 0, 1, 3, 4))
    return (object_grad, probe_grad)
```

```python
import functools
import math

import jax
import jax.numpy as jnp
import ml_dtypes
import numpy as np
from jax import lax
from jax.experimental import pallas as pl
from jax.experimental.pallas import tpu as pltpu
from jax.sharding import PartitionSpec as P

f32 = jnp.float32
bf16 = jnp.bfloat16
MESH = pl.DeviceIdType.MESH
SIDE = 128
PEERS = 16
SLOTS = 4
TILES = 16
ROWS = SLOTS * 32


def signal_all(barrier, targets):
    for target in targets:
        pl.semaphore_signal(barrier, inc=1, device_id=target, device_id_type=MESH)
    pl.semaphore_wait(barrier, len(targets))


def remote(src, dst, send, recv, target):
    return pltpu.make_async_remote_copy(
        src_ref=src, dst_ref=dst, send_sem=send, recv_sem=recv,
        device_id=target, device_id_type=MESH,
    )


def at(pos, tile):
    return {"pos": pos, "tile": tile}


def offset_of(offs, q, j):
    a = offs[q, 0, 2 * j]
    b = offs[q, 0, 2 * j + 1]
    block = lax.div(b, SIDE)
    return a, block, b - block * SIDE


def gather_kernel(off, shard, pieces, offs_out, nxt, own_f, nxt_f, stage, offs, local_sem,
                  off_send, off_recv, nxt_send, nxt_recv, win_send, win_recv):
    me = lax.axis_index("pos")
    tile = lax.axis_index("tile")
    peers = [lax.rem(me + d, PEERS) for d in range(1, PEERS)]
    below = lax.rem(tile + TILES - 1, TILES)
    above = lax.rem(tile + 1, TILES)
    targets = [at(p, tile) for p in peers] + [at(me, below), at(me, above)]
    signal_all(pltpu.get_barrier_semaphore(), targets)

    next_copy = remote(shard, nxt, nxt_send, nxt_recv, at(me, below))
    next_copy.start()
    off_copies = []
    for d in range(1, PEERS):
        copy = remote(off, offs_out.at[me], off_send.at[d], off_recv.at[d], at(peers[d - 1], tile))
        copy.start()
        off_copies.append(copy)
    offs_out[me] = off[...]
    for block in range(8):
        own_f[block] = shard[:, block * SIDE:(block + 1) * SIDE].astype(f32)
    own_f[8] = jnp.zeros((32, SIDE), f32)
    nxt_f[8] = jnp.zeros((32, SIDE), f32)
    for copy in off_copies:
        copy.wait()
    to_smem = pltpu.make_async_copy(offs_out, offs, local_sem)
    to_smem.start()
    next_copy.wait()
    for block in range(8):
        nxt_f[block] = nxt[:, block * SIDE:(block + 1) * SIDE].astype(f32)
    to_smem.wait()

    row = lax.rem(lax.broadcasted_iota(jnp.int32, (32, SIDE), 0), 8) + me * 8
    lane = lax.broadcasted_iota(jnp.int32, (32, SIDE), 1)

    def cut(q):
        for j in range(SLOTS):
            a, block, shift = offset_of(offs, q, j)
            mask = row >= a
            left = jnp.where(mask, own_f[block], nxt_f[block])
            right = jnp.where(mask, own_f[block + 1], nxt_f[block + 1])
            back = lax.rem(SIDE - shift, SIDE)
            both = jnp.where(lane < SIDE - shift, pltpu.roll(left, back, 1), pltpu.roll(right, back, 1))
            stage[q, j * 32:(j + 1) * 32] = both.astype(bf16)

    def window_copy(d):
        q = lax.rem(me + d, PEERS)
        return remote(stage.at[q], pieces.at[me], win_send.at[d], win_recv.at[d], at(q, tile))

    def send(d, carry):
        cut(lax.rem(me + d, PEERS))
        window_copy(d).start()
        return carry

    lax.fori_loop(1, PEERS, send, 0)
    cut(me)
    pieces[me] = stage[me]

    def finish(d, carry):
        window_copy(d).wait()
        return carry

    lax.fori_loop(1, PEERS, finish, 0)


def gather_windows(off, shard):
    vm = pl.BlockSpec(memory_space=pltpu.VMEM)
    dma = pltpu.SemaphoreType.DMA
    return pl.pallas_call(
        gather_kernel,
        out_shape=[
            jax.ShapeDtypeStruct((PEERS, ROWS, SIDE), bf16),
            jax.ShapeDtypeStruct((PEERS, 1, SIDE), jnp.int32),
        ],
        in_specs=[vm, vm],
        out_specs=[vm, vm],
        scratch_shapes=[
            pltpu.VMEM((32, 1024), bf16),
            pltpu.VMEM((9, 32, SIDE), f32),
            pltpu.VMEM((9, 32, SIDE), f32),
            pltpu.VMEM((PEERS, ROWS, SIDE), bf16),
            pltpu.SMEM((PEERS, 1, SIDE), jnp.int32),
            dma, dma((PEERS,)), dma((PEERS,)), dma, dma, dma((PEERS,)), dma((PEERS,)),
        ],
        compiler_params=pltpu.CompilerParams(
            collective_id=0, has_side_effects=True, vmem_limit_bytes=16 << 20
        ),
        name="gather_windows",
    )(off, shard)


def reduce_kernel(offs, gp, probe, out, gout, gin, nacc, nin, cbuf, work, ybuf, work2, xbuf, work3, zbuf,
                  obj_send, obj_recv, nxt_send, nxt_recv, core_send, core_recv,
                  y_send, y_recv, x_send, x_recv, z_send, z_recv):
    me = lax.axis_index("pos")
    tile = lax.axis_index("tile")
    x, zl = lax.div(me, 4), lax.rem(me, 4)
    y, zh, c = lax.div(tile, 4), lax.rem(lax.div(tile, 2), 2), lax.rem(tile, 2)
    z = zh * 4 + zl
    below = lax.rem(tile + TILES - 1, TILES)
    above = lax.rem(tile + 1, TILES)
    partner = at(me, tile + 1 - 2 * c)
    y_of = [lax.rem(y + d, 4) for d in range(4)]
    x_of = [lax.rem(x + d, 4) for d in range(4)]
    z_of = [lax.rem(z + d, 8) for d in range(8)]
    y_peer = [at(me, v * 4 + zh * 2 + c) for v in y_of]
    x_peer = [at(v * 4 + zl, tile) for v in x_of]
    z_peer = [at(x * 4 + lax.rem(v, 4), y * 4 + lax.div(v, 4) * 2 + c) for v in z_of]
    far = [at(x * 4 + d, y * 4 + (1 - zh) * 2 + c) for d in range(4)]
    targets = [at(lax.rem(me + d, PEERS), tile) for d in range(1, PEERS)]
    targets += [at(me, below), at(me, above), partner] + y_peer[1:] + far
    signal_all(pltpu.get_barrier_semaphore(), targets)

    core_copy = remote(probe.at[pl.ds(pl.multiple_of((1 - c) * 1024, 1024), 1024)], cbuf,
                       core_send.at[0], core_recv.at[0], partner)
    core_copy.start()

    def object_copy(d):
        q = lax.rem(me + d, PEERS)
        return remote(gp.at[q], gin.at[d], obj_send.at[d], obj_recv.at[d], at(q, tile))

    def start_object(d, carry):
        object_copy(d).start()
        return carry

    lax.fori_loop(1, PEERS, start_object, 0)
    gin[0] = gp[me]

    def scatter(src, buf, peer, index, size, send, recv, dest, own_size):
        copies = []
        for d in range(1, len(peer)):
            start = pl.multiple_of(index[d] * size, 8)
            copy = remote(src.at[pl.ds(start, size)], buf.at[d - 1], send.at[d], recv.at[d], peer[d])
            copy.start()
            copies.append(copy)
        for copy in copies:
            copy.wait()
        total = src[pl.ds(pl.multiple_of(index[0] * size, 8), size)]
        for d in range(1, len(peer)):
            total = total + buf[d - 1]
        dest[...] = total

    def spread(start, size, peer, send, recv, offset):
        copies = []
        part = gout.at[pl.ds(pl.multiple_of(start, 8), size)]
        for d in range(1, len(peer)):
            copy = remote(part, part, send.at[offset + d], recv.at[offset + d], peer[d])
            copy.start()
            copies.append(copy)
        for copy in copies:
            copy.wait()

    core_copy.wait()
    work[...] = probe[pl.ds(pl.multiple_of(c * 1024, 1024), 1024)] + cbuf[...]
    scatter(work, ybuf, y_peer, y_of, 256, y_send, y_recv, work2, 256)
    scatter(work2, xbuf, x_peer, x_of, 64, x_send, x_recv, work3, 64)
    base = c * 1024
    y_base = base + y * 256
    x_base = y_base + x * 64
    z_base = x_base + z * 8
    scatter(work3, zbuf, z_peer, z_of, 8, z_send, z_recv, gout.at[pl.ds(pl.multiple_of(z_base, 8), 8)], 8)
    spread(z_base, 8, z_peer, z_send, z_recv, 8)

    def finish_object(d, carry):
        object_copy(d).wait()
        return carry

    lax.fori_loop(1, PEERS, finish_object, 0)
    row = lax.broadcasted_iota(jnp.int32, (8, SIDE), 0) + me * 8
    lane = lax.broadcasted_iota(jnp.int32, (8, SIDE), 1)
    for ch in range(4):
        def add(d, acc):
            q = lax.rem(me + PEERS - d, PEERS)
            acc = list(acc)
            for j in range(SLOTS):
                a, block, shift = offset_of(offs, q, j)
                piece = pltpu.roll(gin[d, j * 32 + ch * 8:j * 32 + ch * 8 + 8], shift, 1)
                mine = jnp.where(row >= a, piece, 0.0)
                other = piece - mine
                target = jnp.where(lane < shift, block + 1, block)
                for k in range(8):
                    mask = target == k
                    acc[k] = acc[k] + jnp.where(mask, mine, 0.0)
                    acc[8 + k] = acc[8 + k] + jnp.where(mask, other, 0.0)
            return tuple(acc)

        zero = jnp.zeros((8, SIDE), f32)
        acc = lax.fori_loop(0, PEERS, add, (zero,) * 16)
        for k in range(8):
            out[ch * 8:ch * 8 + 8, k * SIDE:(k + 1) * SIDE] = acc[k]
            nacc[ch * 8:ch * 8 + 8, k * SIDE:(k + 1) * SIDE] = acc[8 + k]
    next_copy = remote(nacc, nin, nxt_send, nxt_recv, at(me, above))
    next_copy.start()
    spread(x_base, 64, x_peer, x_send, x_recv, 4)
    spread(y_base, 256, y_peer, y_send, y_recv, 4)
    half = gout.at[pl.ds(pl.multiple_of(base, 1024), 1024)]
    back_copy = remote(half, half, core_send.at[1], core_recv.at[1], partner)
    back_copy.start()
    next_copy.wait()
    out[...] += nin[...]
    back_copy.wait()


def reduce_all(offs, gp, probe):
    vm = pl.BlockSpec(memory_space=pltpu.VMEM)
    sm = pl.BlockSpec(memory_space=pltpu.SMEM)
    dma = pltpu.SemaphoreType.DMA
    return pl.pallas_call(
        reduce_kernel,
        out_shape=[
            jax.ShapeDtypeStruct((32, 1024), f32),
            jax.ShapeDtypeStruct((2048, SIDE), f32),
        ],
        in_specs=[sm, vm, vm],
        out_specs=[vm, vm],
        scratch_shapes=[
            pltpu.VMEM((PEERS, ROWS, SIDE), f32),
            pltpu.VMEM((32, 1024), f32),
            pltpu.VMEM((32, 1024), f32),
            pltpu.VMEM((1024, SIDE), f32),
            pltpu.VMEM((1024, SIDE), f32),
            pltpu.VMEM((3, 256, SIDE), f32),
            pltpu.VMEM((256, SIDE), f32),
            pltpu.VMEM((3, 64, SIDE), f32),
            pltpu.VMEM((64, SIDE), f32),
            pltpu.VMEM((7, 8, SIDE), f32),
            dma((PEERS,)), dma((PEERS,)), dma, dma, dma((2,)), dma((2,)),
            dma((8,)), dma((8,)), dma((8,)), dma((8,)), dma((16,)), dma((16,)),
        ],
        compiler_params=pltpu.CompilerParams(
            collective_id=1, has_side_effects=True, vmem_limit_bytes=32 << 20
        ),
        name="reduce_all",
    )(offs, gp, probe)


def tables(n):
    k=np.arange(n)
    f=np.exp(-2j*np.pi*(np.outer(k,k)%n)/n)/math.sqrt(n)
    fr=((k+n//2)%n-n//2)/n
    ph=np.exp(-1j*np.pi*24.0*fr**2)
    a=np.conj(f)@(ph[:,None]*f)
    out=[]
    for m in (a,f):
        right=np.block([[m.real,m.imag],[-m.imag,m.real]]).astype(np.float32)
        left=np.block([[m.real,-m.imag],[m.imag,m.real]]).astype(np.float32)
        for t in (right,left):
            hi=t.astype(ml_dtypes.bfloat16)
            lo=(t-hi.astype(np.float32)).astype(ml_dtypes.bfloat16)
            out.append(np.stack([hi,lo]))
    return np.stack(out)

def split(x):
    hi=x.astype(bf16)
    return hi,(x-hi.astype(f32)).astype(bf16)

def dot(a,b):
    return jnp.dot(a,b,preferred_element_type=f32)

def two_sided(tab,which,xr,xi,G):
    x=jnp.concatenate([jnp.concatenate([r,i],axis=1) for r,i in zip(xr,xi)],axis=0)
    h,l=split(x)
    wh,wl=tab[2*which,0],tab[2*which,1]
    z=dot(h,wh)+dot(l,wh)+dot(h,wl)
    P=128
    d=jnp.concatenate([jnp.concatenate([z[m*P:(m+1)*P,c*P:(c+1)*P] for m in range(G)],axis=1) for c in range(2)],axis=0)
    h,l=split(d)
    wh,wl=tab[2*which+1,0],tab[2*which+1,1]
    o=dot(wh,h)+dot(wh,l)+dot(wl,h)
    return [o[:P,m*P:(m+1)*P] for m in range(G)],[o[P:,m*P:(m+1)*P] for m in range(G)]

def kernel(G,M,S,offs,cnt,pieces,probe,pat,tab,gp,gprobe,dbl,win,phi,psi,inten):
    P=128
    for m in range(M):
        for c in range(2):
            gprobe[m,c]=jnp.zeros((P,P),f32)
    gp[...]=jnp.zeros(gp.shape,f32)
    def slot(j,_):
        a=offs[j,0]
        for ch in range(4):
            for p in range(16):
                start=pl.multiple_of(j*32+(ch//2)*16,16)
                v=pieces[p,pl.ds(start,16),:].astype(f32)[(ch%2)*8:(ch%2)*8+8]
                dbl[ch,p*8:p*8+8]=v
                dbl[ch,P+p*8:P+p*8+8]=v
        for ch in range(4):
            win[ch]=dbl[ch,pl.ds(a,P),:]
        inten[...]=-pat[j]
        def fwd(i,_):
            m0=i*G
            w0r,w0i=win[0],win[1]
            xr=[];xi=[]
            for g in range(G):
                pr,pi=probe[m0+g,0],probe[m0+g,1]
                xr.append(pr*w0r-pi*w0i); xi.append(pr*w0i+pi*w0r)
            zr,zi=two_sided(tab,0,xr,xi,G)
            w1r,w1i=win[2],win[3]
            xr=[];xi=[]
            for g in range(G):
                phi[m0+g,0]=zr[g]; phi[m0+g,1]=zi[g]
                xr.append(zr[g]*w1r-zi[g]*w1i); xi.append(zr[g]*w1i+zi[g]*w1r)
            zr,zi=two_sided(tab,1,xr,xi,G)
            acc=inten[...]
            for g in range(G):
                psi[m0+g,0]=zr[g]; psi[m0+g,1]=zi[g]
                acc=acc+zr[g]*zr[g]+zi[g]*zi[g]
            inten[...]=acc
            return 0
        lax.fori_loop(0,M//G,fwd,0)
        for ch in range(4):
            dbl[ch,:P]=jnp.zeros((P,P),f32)
        def bwd(i,_):
            m0=i*G
            res=2.0*inten[...]
            xr=[];xi=[]
            for g in range(G):
                xr.append(psi[m0+g,0]*res); xi.append(psi[m0+g,1]*-res)
            zr,zi=two_sided(tab,1,xr,xi,G)
            w1r,w1i=win[2],win[3]
            ar=dbl[2,:P]; ai=dbl[3,:P]
            xr=[];xi=[]
            for g in range(G):
                fr,fi=phi[m0+g,0],phi[m0+g,1]
                ar=ar+(fr*zr[g]-fi*zi[g]); ai=ai-(fr*zi[g]+fi*zr[g])
                xr.append(zr[g]*w1r-zi[g]*w1i); xi.append(zr[g]*w1i+zi[g]*w1r)
            dbl[2,:P]=ar; dbl[3,:P]=ai
            zr,zi=two_sided(tab,0,xr,xi,G)
            w0r,w0i=win[0],win[1]
            ar=dbl[0,:P]; ai=dbl[1,:P]
            for g in range(G):
                pr,pi=probe[m0+g,0],probe[m0+g,1]
                ar=ar+(pr*zr[g]-pi*zi[g]); ai=ai-(pr*zi[g]+pi*zr[g])
                gprobe[m0+g,0]+=zr[g]*w0r-zi[g]*w0i
                gprobe[m0+g,1]-=zr[g]*w0i+zi[g]*w0r
            dbl[0,:P]=ar; dbl[1,:P]=ai
            return 0
        lax.fori_loop(0,M//G,bwd,0)
        for ch in range(4):
            dbl[ch,P:]=dbl[ch,:P]
        for ch in range(4):
            r=dbl[ch,pl.ds(P-a,P),:]
            for p in range(16):
                start=pl.multiple_of(j*32+ch*8,8)
                gp[p,pl.ds(start,8),:]=r[p*8:p*8+8]
        return 0
    lax.fori_loop(0,cnt[0,0],slot,0)

def compute(offs,cnt,pieces,probe,pat,tab,G=2):
    M,S=probe.shape[0],pat.shape[0]
    sm=pl.BlockSpec(memory_space=pltpu.SMEM); vm=pl.BlockSpec(memory_space=pltpu.VMEM)
    return pl.pallas_call(functools.partial(kernel,G,M,S),
        out_shape=[jax.ShapeDtypeStruct((16,S*32,128),f32),jax.ShapeDtypeStruct(probe.shape,f32)],
        in_specs=[sm,sm,vm,vm,vm,vm],out_specs=[vm,vm],
        scratch_shapes=[pltpu.VMEM((4,256,128),f32),pltpu.VMEM((4,128,128),f32),
            pltpu.VMEM((M,2,128,128),f32),pltpu.VMEM((M,2,128,128),f32),pltpu.VMEM((128,128),f32)],
        compiler_params=pltpu.CompilerParams(vmem_limit_bytes=48<<20),name="ptycho")(offs,cnt,pieces,probe,pat,tab)


def per_device(object_slices, probe_modes, offsets, counts, patterns):
    shard = object_slices.reshape(32, 1024)
    off = jnp.pad(offsets.reshape(1, 2 * SLOTS), ((0, 0), (0, SIDE - 2 * SLOTS)))
    pieces, offs = gather_windows(off, shard)
    gp, gprobe = compute(offsets[0, 0], counts, pieces, probe_modes, patterns[0, 0], jnp.asarray(tables(SIDE)), 8)
    out, gout = reduce_all(offs, gp, gprobe.reshape(2048, SIDE))
    return out.reshape(object_slices.shape), gout.reshape(probe_modes.shape)


def solution(mesh):
    placed = (
        P("tile", None, None, "pos", None),
        P(),
        P("tile", "pos", None, None),
        P("tile", "pos"),
        P("tile", "pos", None, None, None),
    )
    return jax.shard_map(
        per_device,
        mesh=mesh,
        in_specs=placed,
        out_specs=(P("tile", None, None, "pos", None), P()),
        check_vma=False,
    )
```

```python
import functools
import math

import jax
import jax.numpy as jnp
import ml_dtypes
import numpy as np
from jax import lax
from jax.experimental import pallas as pl
from jax.experimental.pallas import tpu as pltpu
from jax.sharding import PartitionSpec as P

f32 = jnp.float32
bf16 = jnp.bfloat16
MESH = pl.DeviceIdType.MESH
SIDE = 128
PEERS = 16
SLOTS = 4
TILES = 16
MODES = 8


def signal_all(barrier, targets):
    for target in targets:
        pl.semaphore_signal(barrier, inc=1, device_id=target, device_id_type=MESH)
    pl.semaphore_wait(barrier, len(targets))


def remote(src, dst, send, recv, target):
    return pltpu.make_async_remote_copy(
        src_ref=src, dst_ref=dst, send_sem=send, recv_sem=recv,
        device_id=target, device_id_type=MESH,
    )


def at(pos, tile):
    return {"pos": pos, "tile": tile}


def offset_of(offs, q, j):
    a = offs[q, 0, 2 * j]
    b = offs[q, 0, 2 * j + 1]
    block = lax.div(b, SIDE)
    return a, block, b - block * SIDE


def tables(n):
    k=np.arange(n)
    f=np.exp(-2j*np.pi*(np.outer(k,k)%n)/n)/math.sqrt(n)
    fr=((k+n//2)%n-n//2)/n
    ph=np.exp(-1j*np.pi*24.0*fr**2)
    a=np.conj(f)@(ph[:,None]*f)
    out=[]
    for m in (a,f):
        right=np.block([[m.real,m.imag],[-m.imag,m.real]]).astype(np.float32)
        left=np.block([[m.real,-m.imag],[m.imag,m.real]]).astype(np.float32)
        for t in (right,left):
            hi=t.astype(ml_dtypes.bfloat16)
            lo=(t-hi.astype(np.float32)).astype(ml_dtypes.bfloat16)
            out.append(np.stack([hi,lo]))
    return np.stack(out)

def split(x):
    hi=x.astype(bf16)
    return hi,(x-hi.astype(f32)).astype(bf16)

def dot(a,b):
    return jnp.dot(a,b,preferred_element_type=f32)

def two_sided(tab,which,xr,xi,G):
    x=jnp.concatenate([jnp.concatenate([r,i],axis=1) for r,i in zip(xr,xi)],axis=0)
    h,l=split(x)
    wh,wl=tab[2*which,0],tab[2*which,1]
    z=dot(h,wh)+dot(l,wh)+dot(h,wl)
    P=128
    d=jnp.concatenate([jnp.concatenate([z[m*P:(m+1)*P,c*P:(c+1)*P] for m in range(G)],axis=1) for c in range(2)],axis=0)
    h,l=split(d)
    wh,wl=tab[2*which+1,0],tab[2*which+1,1]
    o=dot(wh,h)+dot(wh,l)+dot(wl,h)
    return [o[:P,m*P:(m+1)*P] for m in range(G)],[o[P:,m*P:(m+1)*P] for m in range(G)]


def fused_kernel(off, cnt, shard, probe_hbm, pat_hbm, tab_hbm, out, gout,
                 probe, pat, tab, nxt, own_f, nxt_f, wstage, pieces, offs_v, offs,
                 dbl, win, phi, psi, inten, gprobe, gp, gin, nacc, nin,
                 cbuf, work, xybuf, zbuf,
                 local_sem, off_send, off_recv, nxt_send, nxt_recv, win_send, win_recv,
                 obj_send, obj_recv, core_send, core_recv, xy_send, xy_recv, z_send, z_recv):
    me = lax.axis_index("pos")
    tile = lax.axis_index("tile")
    x, zl = lax.div(me, 4), lax.rem(me, 4)
    y, zh, c = lax.div(tile, 4), lax.rem(lax.div(tile, 2), 2), lax.rem(tile, 2)
    z = zh * 4 + zl
    index = y * 4 + x
    below = lax.rem(tile + TILES - 1, TILES)
    above = lax.rem(tile + 1, TILES)
    partner = at(me, tile + 1 - 2 * c)

    def xy_peer(d):
        px, py = lax.rem(x + lax.rem(d, 4), 4), lax.rem(y + lax.div(d, 4), 4)
        return py * 4 + px, at(px * 4 + zl, py * 4 + zh * 2 + c)

    def z_peer(d):
        pz = lax.rem(z + d, 8)
        return at(x * 4 + lax.rem(pz, 4), y * 4 + lax.div(pz, 4) * 2 + c)

    loads = [
        pltpu.make_async_copy(probe_hbm, probe, local_sem.at[0]),
        pltpu.make_async_copy(tab_hbm, tab, local_sem.at[1]),
        pltpu.make_async_copy(pat_hbm, pat, local_sem.at[2]),
    ]
    for load in loads:
        load.start()
    targets = [at(lax.rem(me + d, PEERS), tile) for d in range(1, PEERS)]
    targets += [xy_peer(d)[1] for d in range(4, PEERS)]
    targets += [at(x * 4 + d, y * 4 + (1 - zh) * 2 + c) for d in range(4)]
    targets += [at(me, below), at(me, above), partner]
    signal_all(pltpu.get_barrier_semaphore(), targets)

    first_next = remote(shard, nxt, nxt_send.at[0], nxt_recv.at[0], at(me, below))
    first_next.start()

    def off_copy(d):
        return remote(off, offs_v.at[me], off_send.at[d], off_recv.at[d], at(lax.rem(me + d, PEERS), tile))

    def each_peer(action):
        def step(d, carry):
            action(d)
            return carry

        lax.fori_loop(1, PEERS, step, 0)

    each_peer(lambda d: off_copy(d).start())
    offs_v[me] = off[...]
    for block in range(8):
        own_f[block] = shard[:, block * SIDE:(block + 1) * SIDE].astype(f32)
    own_f[8] = jnp.zeros((32, SIDE), f32)
    nxt_f[8] = jnp.zeros((32, SIDE), f32)
    gprobe[...] = jnp.zeros(gprobe.shape, f32)
    out[...] = jnp.zeros(out.shape, f32)
    nacc[...] = jnp.zeros(nacc.shape, f32)
    each_peer(lambda d: off_copy(d).wait())
    to_smem = pltpu.make_async_copy(offs_v, offs, local_sem.at[3])
    to_smem.start()
    first_next.wait()
    for block in range(8):
        nxt_f[block] = nxt[:, block * SIDE:(block + 1) * SIDE].astype(f32)
    to_smem.wait()

    row32 = lax.rem(lax.broadcasted_iota(jnp.int32, (32, SIDE), 0), 8) + me * 8
    lane32 = lax.broadcasted_iota(jnp.int32, (32, SIDE), 1)

    def cut(q, j):
        a, block, shift = offset_of(offs, q, j)
        mask = row32 >= a
        left = jnp.where(mask, own_f[block], nxt_f[block])
        right = jnp.where(mask, own_f[block + 1], nxt_f[block + 1])
        back = lax.rem(SIDE - shift, SIDE)
        both = jnp.where(lane32 < SIDE - shift, pltpu.roll(left, back, 1), pltpu.roll(right, back, 1))
        return both.astype(bf16)

    def window_copy(j, d):
        q = lax.rem(me + d, PEERS)
        return remote(wstage.at[j, q], pieces.at[j, me], win_send.at[j, d], win_recv.at[j, d], at(q, tile))

    def send_windows(j, carry):
        def send(d):
            q = lax.rem(me + d, PEERS)
            wstage[j, q] = cut(q, j)
            window_copy(j, d).start()

        each_peer(send)
        pieces[j, me] = cut(me, j)
        return carry

    lax.fori_loop(0, SLOTS, send_windows, 0)

    def object_copy(j, d):
        q = lax.rem(me + d, PEERS)
        return remote(gp.at[j, q], gin.at[j, d], obj_send.at[j, d], obj_recv.at[j, d], at(q, tile))

    for load in loads:
        load.wait()
    live_count = cnt[0, 0]

    def slot(j, carry):
        each_peer(lambda d: window_copy(j, d).wait())
        a = offs[me, 0, 2 * j]
        for p in range(PEERS):
            piece = pieces[j, p].astype(f32)
            for ch in range(4):
                part = piece[ch * 8:ch * 8 + 8]
                dbl[ch, p * 8:p * 8 + 8] = part
                dbl[ch, SIDE + p * 8:SIDE + p * 8 + 8] = part
        for ch in range(4):
            win[ch] = dbl[ch, pl.ds(a, SIDE), :]
        w0r, w0i = win[0], win[1]
        xr, xi = [], []
        for m in range(MODES):
            pr, pi = probe[m, 0], probe[m, 1]
            xr.append(pr * w0r - pi * w0i)
            xi.append(pr * w0i + pi * w0r)
        zr, zi = two_sided(tab, 0, xr, xi, MODES)
        w1r, w1i = win[2], win[3]
        xr, xi = [], []
        for m in range(MODES):
            phi[m, 0] = zr[m]
            phi[m, 1] = zi[m]
            xr.append(zr[m] * w1r - zi[m] * w1i)
            xi.append(zr[m] * w1i + zi[m] * w1r)
        zr, zi = two_sided(tab, 1, xr, xi, MODES)
        total = -pat[j]
        for m in range(MODES):
            psi[m, 0] = zr[m]
            psi[m, 1] = zi[m]
            total = total + zr[m] * zr[m] + zi[m] * zi[m]
        slot_number = jnp.zeros((SIDE, SIDE), jnp.int32) + j
        inten[...] = jnp.where(slot_number < live_count, 2.0 * total, 0.0)

        res = inten[...]
        xr, xi = [], []
        for m in range(MODES):
            xr.append(psi[m, 0] * res)
            xi.append(psi[m, 1] * -res)
        zr, zi = two_sided(tab, 1, xr, xi, MODES)
        w1r, w1i = win[2], win[3]
        ar = ai = jnp.zeros((SIDE, SIDE), f32)
        xr, xi = [], []
        for m in range(MODES):
            fr, fi = phi[m, 0], phi[m, 1]
            ar = ar + (fr * zr[m] - fi * zi[m])
            ai = ai - (fr * zi[m] + fi * zr[m])
            xr.append(zr[m] * w1r - zi[m] * w1i)
            xi.append(zr[m] * w1i + zi[m] * w1r)
        for half in range(2):
            dbl[2, half * SIDE:(half + 1) * SIDE] = ar
            dbl[3, half * SIDE:(half + 1) * SIDE] = ai
        zr, zi = two_sided(tab, 0, xr, xi, MODES)
        w0r, w0i = win[0], win[1]
        ar = ai = jnp.zeros((SIDE, SIDE), f32)
        for m in range(MODES):
            pr, pi = probe[m, 0], probe[m, 1]
            ar = ar + (pr * zr[m] - pi * zi[m])
            ai = ai - (pr * zi[m] + pi * zr[m])
            gprobe[8 * m:8 * m + 4] += (zr[m] * w0r - zi[m] * w0i).reshape(4, 32, SIDE)
            gprobe[8 * m + 4:8 * m + 8] -= (zr[m] * w0i + zi[m] * w0r).reshape(4, 32, SIDE)
        for half in range(2):
            dbl[0, half * SIDE:(half + 1) * SIDE] = ar
            dbl[1, half * SIDE:(half + 1) * SIDE] = ai
        for ch in range(4):
            rolled = dbl[ch, pl.ds(SIDE - a, SIDE), :]
            for p in range(PEERS):
                gp[j, p, ch * 8:ch * 8 + 8] = rolled[p * 8:p * 8 + 8]
        each_peer(lambda d: object_copy(j, d).start())
        gin[j, 0] = gp[j, me]
        return carry

    lax.fori_loop(0, SLOTS, slot, 0)

    def core_copy(k):
        src = gprobe.at[pl.ds(32 * k + 16 * (1 - c), 16)]
        return remote(src, cbuf.at[k], core_send.at[k], core_recv.at[k], partner)

    def xy_copy(k, d):
        i, peer = xy_peer(d)
        return remote(work.at[k, i], xybuf.at[k, d], xy_send.at[k, d], xy_recv.at[k, d], peer)

    def z_copy(k, d):
        part = zbuf.at[k, z]
        return remote(part, part, z_send.at[k, d], z_recv.at[k, d], z_peer(d))

    def xy_back(k, d):
        part = gout.at[32 * k + 16 * c + index]
        return remote(part, part, xy_send.at[2 + k, d], xy_recv.at[2 + k, d], xy_peer(d)[1])

    def core_back(k):
        part = gout.at[pl.ds(32 * k + 16 * c, 16)]
        return remote(part, part, core_send.at[2 + k], core_recv.at[2 + k], partner)

    row8 = lax.broadcasted_iota(jnp.int32, (8, SIDE), 0) + me * 8
    lane8 = lax.broadcasted_iota(jnp.int32, (8, SIDE), 1)

    def accumulate(slots):
        for ch in range(4):
            def add(d, acc):
                q = lax.rem(me + PEERS - d, PEERS)
                acc = list(acc)
                for j in slots:
                    a, block, shift = offset_of(offs, q, j)
                    piece = pltpu.roll(gin[j, d, ch * 8:ch * 8 + 8], shift, 1)
                    mine = jnp.where(row8 >= a, piece, 0.0)
                    other = piece - mine
                    target = jnp.where(lane8 < shift, block + 1, block)
                    for k in range(8):
                        mask = target == k
                        acc[k] = acc[k] + jnp.where(mask, mine, 0.0)
                        acc[8 + k] = acc[8 + k] + jnp.where(mask, other, 0.0)
                return tuple(acc)

            cols = [slice(k * SIDE, (k + 1) * SIDE) for k in range(8)]
            rows = slice(ch * 8, ch * 8 + 8)
            acc = [out[rows, s] for s in cols] + [nacc[rows, s] for s in cols]
            acc = lax.fori_loop(0, PEERS, add, tuple(acc))
            for k in range(8):
                out[rows, cols[k]] = acc[k]
                nacc[rows, cols[k]] = acc[8 + k]

    for k in range(2):
        core_copy(k).start()
    for k in range(2):
        core_copy(k).wait()
        work[k] = gprobe[pl.ds(32 * k + 16 * c, 16)] + cbuf[k]
        each_peer(lambda d: xy_copy(k, d).start())
    for j in range(SLOTS - 1):
        each_peer(lambda d: object_copy(j, d).wait())
    accumulate(range(SLOTS - 1))
    each_peer(lambda d: object_copy(SLOTS - 1, d).wait())
    accumulate(range(SLOTS - 1, SLOTS))
    last_next = remote(nacc, nin, nxt_send.at[1], nxt_recv.at[1], at(me, above))
    last_next.start()
    for k in range(2):
        each_peer(lambda d: xy_copy(k, d).wait())
        total = work[k, index]
        for d in range(1, PEERS):
            total = total + xybuf[k, d]
        zbuf[k, z] = total
        for d in range(1, 8):
            z_copy(k, d).start()
    for k in range(2):
        for d in range(1, 8):
            z_copy(k, d).wait()
        total = zbuf[k, 0]
        for d in range(1, 8):
            total = total + zbuf[k, d]
        gout[32 * k + 16 * c + index] = total
        each_peer(lambda d: xy_back(k, d).start())
    for k in range(2):
        each_peer(lambda d: xy_back(k, d).wait())
        core_back(k).start()
    last_next.wait()
    out[...] += nin[...]
    for k in range(2):
        core_back(k).wait()


def fused(off, cnt, shard, probe, pat, tab):
    vm = pl.BlockSpec(memory_space=pltpu.VMEM)
    sm = pl.BlockSpec(memory_space=pltpu.SMEM)
    hbm = pl.BlockSpec(memory_space=pl.ANY)
    dma = pltpu.SemaphoreType.DMA
    vmem = pltpu.VMEM
    return pl.pallas_call(
        fused_kernel,
        out_shape=[
            jax.ShapeDtypeStruct((32, 1024), f32),
            jax.ShapeDtypeStruct((64, 32, SIDE), f32),
        ],
        in_specs=[vm, sm, vm, hbm, hbm, hbm],
        out_specs=[vm, vm],
        scratch_shapes=[
            vmem((MODES, 2, SIDE, SIDE), f32),
            vmem((SLOTS, SIDE, SIDE), f32),
            vmem((4, 2, 256, 256), bf16),
            vmem((32, 1024), bf16),
            vmem((9, 32, SIDE), f32),
            vmem((9, 32, SIDE), f32),
            vmem((SLOTS, PEERS, 32, SIDE), bf16),
            vmem((SLOTS, PEERS, 32, SIDE), bf16),
            vmem((PEERS, 1, SIDE), jnp.int32),
            pltpu.SMEM((PEERS, 1, SIDE), jnp.int32),
            vmem((4, 256, SIDE), f32),
            vmem((4, SIDE, SIDE), f32),
            vmem((MODES, 2, SIDE, SIDE), f32),
            vmem((MODES, 2, SIDE, SIDE), f32),
            vmem((SIDE, SIDE), f32),
            vmem((64, 32, SIDE), f32),
            vmem((SLOTS, PEERS, 32, SIDE), f32),
            vmem((SLOTS, PEERS, 32, SIDE), f32),
            vmem((32, 1024), f32),
            vmem((32, 1024), f32),
            vmem((2, 16, 32, SIDE), f32),
            vmem((2, 16, 32, SIDE), f32),
            vmem((2, 16, 32, SIDE), f32),
            vmem((2, 8, 32, SIDE), f32),
            dma((4,)), dma((PEERS,)), dma((PEERS,)), dma((2,)), dma((2,)),
            dma((SLOTS, PEERS)), dma((SLOTS, PEERS)), dma((SLOTS, PEERS)), dma((SLOTS, PEERS)),
            dma((4,)), dma((4,)), dma((4, PEERS)), dma((4, PEERS)), dma((2, 8)), dma((2, 8)),
        ],
        compiler_params=pltpu.CompilerParams(
            collective_id=0, has_side_effects=True, vmem_limit_bytes=48 << 20
        ),
        name="ptychography",
    )(off, cnt, shard, probe, pat, tab)


def per_device(object_slices, probe_modes, offsets, counts, patterns):
    shard = object_slices.reshape(32, 1024)
    off = jnp.pad(offsets.reshape(1, 2 * SLOTS), ((0, 0), (0, SIDE - 2 * SLOTS)))
    out, gout = fused(off, counts, shard, probe_modes, patterns[0, 0], jnp.asarray(tables(SIDE)))
    return out.reshape(object_slices.shape), gout.reshape(probe_modes.shape)


def solution(mesh):
    placed = (
        P("tile", None, None, "pos", None),
        P(),
        P("tile", "pos", None, None),
        P("tile", "pos"),
        P("tile", "pos", None, None, None),
    )
    return jax.shard_map(
        per_device,
        mesh=mesh,
        in_specs=placed,
        out_specs=(P("tile", None, None, "pos", None), P()),
        check_vma=False,
    )
```

```python
import functools
import math

import jax
import jax.numpy as jnp
import ml_dtypes
import numpy as np
from jax import lax
from jax.experimental import pallas as pl
from jax.experimental.pallas import tpu as pltpu
from jax.sharding import PartitionSpec as P

f32 = jnp.float32
bf16 = jnp.bfloat16
MESH = pl.DeviceIdType.MESH
SIDE = 128
PEERS = 16
SLOTS = 4
TILES = 16
MODES = 8


def signal_all(barrier, targets):
    for target in targets:
        pl.semaphore_signal(barrier, inc=1, device_id=target, device_id_type=MESH)
    pl.semaphore_wait(barrier, len(targets))


def remote(src, dst, send, recv, target):
    return pltpu.make_async_remote_copy(
        src_ref=src, dst_ref=dst, send_sem=send, recv_sem=recv,
        device_id=target, device_id_type=MESH,
    )


def at(pos, tile):
    return {"pos": pos, "tile": tile}


def offset_of(offs, q, j):
    a = offs[q, 0, 2 * j]
    b = offs[q, 0, 2 * j + 1]
    block = lax.div(b, SIDE)
    return a, block, b - block * SIDE


def tables(n):
    k=np.arange(n)
    f=np.exp(-2j*np.pi*(np.outer(k,k)%n)/n)/math.sqrt(n)
    fr=((k+n//2)%n-n//2)/n
    ph=np.exp(-1j*np.pi*24.0*fr**2)
    a=np.conj(f)@(ph[:,None]*f)
    out=[]
    for m in (a,f):
        right=np.block([[m.real,m.imag],[-m.imag,m.real]]).astype(np.float32)
        left=np.block([[m.real,-m.imag],[m.imag,m.real]]).astype(np.float32)
        for t in (right,left):
            hi=t.astype(ml_dtypes.bfloat16)
            lo=(t-hi.astype(np.float32)).astype(ml_dtypes.bfloat16)
            out.append(np.stack([hi,lo]))
    return np.stack(out)

def split(x):
    hi=x.astype(bf16)
    return hi,(x-hi.astype(f32)).astype(bf16)

def dot(a,b):
    return jnp.dot(a,b,preferred_element_type=f32)


def two_sided(tab, which, xr, xi):
    right_hi, right_lo = tab[2 * which, 0], tab[2 * which, 1]
    left_hi, left_lo = tab[2 * which + 1, 0], tab[2 * which + 1, 1]
    halves = []
    for m in range(0, MODES, 2):
        rows = [jnp.concatenate([xr[i], xi[i]], axis=1) for i in (m, m + 1)]
        hi, lo = split(jnp.concatenate(rows, axis=0))
        z = dot(hi, right_hi) + dot(lo, right_hi) + dot(hi, right_lo)
        top = jnp.concatenate([z[:SIDE, :SIDE], z[SIDE:, :SIDE]], axis=1)
        bottom = jnp.concatenate([z[:SIDE, SIDE:], z[SIDE:, SIDE:]], axis=1)
        halves.append(jnp.concatenate([top, bottom], axis=0))
    real, imag = [], []
    for half in halves:
        hi, lo = split(half)
        o = dot(left_hi, hi) + dot(left_hi, lo) + dot(left_lo, hi)
        real += [o[:SIDE, :SIDE], o[:SIDE, SIDE:]]
        imag += [o[SIDE:, :SIDE], o[SIDE:, SIDE:]]
    return real, imag


def fused_kernel(off_in, cnt, shard, probe_hbm, pat_hbm, tab_hbm, out, gout,
                 off, probe, pat, tab, nxt, own_f, nxt_f, wstage, pieces, offs_v, offs,
                 dbl, win, phi, psi, inten, gprobe, gp, gin, nacc, nin,
                 cbuf, work, xybuf, zbuf,
                 local_sem, off_send, off_recv, nxt_send, nxt_recv, win_send, win_recv,
                 obj_send, obj_recv, core_send, core_recv, xy_send, xy_recv, z_send, z_recv):
    me = lax.axis_index("pos")
    tile = lax.axis_index("tile")
    x, zl = lax.div(me, 4), lax.rem(me, 4)
    y, zh, c = lax.div(tile, 4), lax.rem(lax.div(tile, 2), 2), lax.rem(tile, 2)
    z = zh * 4 + zl
    index = y * 4 + x
    below = lax.rem(tile + TILES - 1, TILES)
    above = lax.rem(tile + 1, TILES)
    partner = at(me, tile + 1 - 2 * c)

    def xy_peer(d):
        px, py = lax.rem(x + lax.rem(d, 4), 4), lax.rem(y + lax.div(d, 4), 4)
        return py * 4 + px, at(px * 4 + zl, py * 4 + zh * 2 + c)

    def z_peer(d):
        pz = lax.rem(z + d, 8)
        return at(x * 4 + lax.rem(pz, 4), y * 4 + lax.div(pz, 4) * 2 + c)

    loads = [
        pltpu.make_async_copy(probe_hbm, probe, local_sem.at[0]),
        pltpu.make_async_copy(tab_hbm, tab, local_sem.at[1]),
        pltpu.make_async_copy(pat_hbm, pat, local_sem.at[2]),
    ]
    for load in loads:
        load.start()
    lane1 = lax.broadcasted_iota(jnp.int32, (1, SIDE), 1)
    row = jnp.zeros((1, SIDE), jnp.int32)
    for j in range(SLOTS):
        for i in range(2):
            row = jnp.where(lane1 == 2 * j + i, off_in[i, j], row)
    off[...] = row
    offs_v[me] = row
    targets = [at(lax.rem(me + d, PEERS), tile) for d in range(1, PEERS)]
    targets += [xy_peer(d)[1] for d in range(4, PEERS)]
    targets += [at(x * 4 + d, y * 4 + (1 - zh) * 2 + c) for d in range(4)]
    targets += [at(me, below), at(me, above), partner]
    signal_all(pltpu.get_barrier_semaphore(), targets)

    first_next = remote(shard, nxt, nxt_send.at[0], nxt_recv.at[0], at(me, below))
    first_next.start()

    def off_copy(d):
        return remote(off, offs_v.at[me], off_send.at[d], off_recv.at[d], at(lax.rem(me + d, PEERS), tile))

    def each_peer(action):
        def step(d, carry):
            action(d)
            return carry

        lax.fori_loop(1, PEERS, step, 0)

    each_peer(lambda d: off_copy(d).start())
    for block in range(8):
        own_f[block] = shard[:, block * SIDE:(block + 1) * SIDE].astype(f32)
    own_f[8] = jnp.zeros((32, SIDE), f32)
    nxt_f[8] = jnp.zeros((32, SIDE), f32)
    gprobe[...] = jnp.zeros(gprobe.shape, f32)
    out[...] = jnp.zeros(out.shape, f32)
    nacc[...] = jnp.zeros(nacc.shape, f32)
    each_peer(lambda d: off_copy(d).wait())
    to_smem = pltpu.make_async_copy(offs_v, offs, local_sem.at[3])
    to_smem.start()
    first_next.wait()
    for block in range(8):
        nxt_f[block] = nxt[:, block * SIDE:(block + 1) * SIDE].astype(f32)
    to_smem.wait()

    row32 = lax.rem(lax.broadcasted_iota(jnp.int32, (32, SIDE), 0), 8) + me * 8
    lane32 = lax.broadcasted_iota(jnp.int32, (32, SIDE), 1)

    def cut(q, j):
        a, block, shift = offset_of(offs, q, j)
        mask = row32 >= a
        left = jnp.where(mask, own_f[block], nxt_f[block])
        right = jnp.where(mask, own_f[block + 1], nxt_f[block + 1])
        back = lax.rem(SIDE - shift, SIDE)
        both = jnp.where(lane32 < SIDE - shift, pltpu.roll(left, back, 1), pltpu.roll(right, back, 1))
        return both.astype(bf16)

    def window_copy(j, d):
        q = lax.rem(me + d, PEERS)
        return remote(wstage.at[j, q], pieces.at[j, me], win_send.at[j, d], win_recv.at[j, d], at(q, tile))

    def send_windows(j, carry):
        def send(d):
            q = lax.rem(me + d, PEERS)
            wstage[j, q] = cut(q, j)
            window_copy(j, d).start()

        each_peer(send)
        pieces[j, me] = cut(me, j)
        return carry

    lax.fori_loop(0, SLOTS, send_windows, 0)

    def object_copy(j, d):
        q = lax.rem(me + d, PEERS)
        return remote(gp.at[j, q], gin.at[j, d], obj_send.at[j, d], obj_recv.at[j, d], at(q, tile))

    for load in loads:
        load.wait()
    live_count = cnt[0, 0]

    def slot(j, carry):
        each_peer(lambda d: window_copy(j, d).wait())
        a = offs[me, 0, 2 * j]
        for p in range(PEERS):
            piece = pieces[j, p].astype(f32)
            for ch in range(4):
                part = piece[ch * 8:ch * 8 + 8]
                dbl[ch, p * 8:p * 8 + 8] = part
                dbl[ch, SIDE + p * 8:SIDE + p * 8 + 8] = part
        for ch in range(4):
            win[ch] = dbl[ch, pl.ds(a, SIDE), :]
        w0r, w0i = win[0], win[1]
        xr, xi = [], []
        for m in range(MODES):
            pr, pi = probe[m, 0], probe[m, 1]
            xr.append(pr * w0r - pi * w0i)
            xi.append(pr * w0i + pi * w0r)
        zr, zi = two_sided(tab, 0, xr, xi)
        w1r, w1i = win[2], win[3]
        xr, xi = [], []
        for m in range(MODES):
            phi[m, 0] = zr[m]
            phi[m, 1] = zi[m]
            xr.append(zr[m] * w1r - zi[m] * w1i)
            xi.append(zr[m] * w1i + zi[m] * w1r)
        zr, zi = two_sided(tab, 1, xr, xi)
        total = -pat[j]
        for m in range(MODES):
            psi[m, 0] = zr[m]
            psi[m, 1] = zi[m]
            total = total + zr[m] * zr[m] + zi[m] * zi[m]
        slot_number = jnp.zeros((SIDE, SIDE), jnp.int32) + j
        inten[...] = jnp.where(slot_number < live_count, 2.0 * total, 0.0)

        res = inten[...]
        xr, xi = [], []
        for m in range(MODES):
            xr.append(psi[m, 0] * res)
            xi.append(psi[m, 1] * -res)
        zr, zi = two_sided(tab, 1, xr, xi)
        w1r, w1i = win[2], win[3]
        ar = ai = jnp.zeros((SIDE, SIDE), f32)
        xr, xi = [], []
        for m in range(MODES):
            fr, fi = phi[m, 0], phi[m, 1]
            ar = ar + (fr * zr[m] - fi * zi[m])
            ai = ai - (fr * zi[m] + fi * zr[m])
            xr.append(zr[m] * w1r - zi[m] * w1i)
            xi.append(zr[m] * w1i + zi[m] * w1r)
        for half in range(2):
            dbl[2, half * SIDE:(half + 1) * SIDE] = ar
            dbl[3, half * SIDE:(half + 1) * SIDE] = ai
        zr, zi = two_sided(tab, 0, xr, xi)
        w0r, w0i = win[0], win[1]
        ar = ai = jnp.zeros((SIDE, SIDE), f32)
        for m in range(MODES):
            pr, pi = probe[m, 0], probe[m, 1]
            ar = ar + (pr * zr[m] - pi * zi[m])
            ai = ai - (pr * zi[m] + pi * zr[m])
            gprobe[8 * m:8 * m + 4] += (zr[m] * w0r - zi[m] * w0i).reshape(4, 32, SIDE)
            gprobe[8 * m + 4:8 * m + 8] -= (zr[m] * w0i + zi[m] * w0r).reshape(4, 32, SIDE)
        for half in range(2):
            dbl[0, half * SIDE:(half + 1) * SIDE] = ar
            dbl[1, half * SIDE:(half + 1) * SIDE] = ai
        for ch in range(4):
            rolled = dbl[ch, pl.ds(SIDE - a, SIDE), :]
            for p in range(PEERS):
                gp[j, p, ch * 8:ch * 8 + 8] = rolled[p * 8:p * 8 + 8]
        each_peer(lambda d: object_copy(j, d).start())
        gin[j, 0] = gp[j, me]
        return carry

    lax.fori_loop(0, SLOTS, slot, 0)

    def core_copy(k):
        src = gprobe.at[pl.ds(32 * k + 16 * (1 - c), 16)]
        return remote(src, cbuf.at[k], core_send.at[k], core_recv.at[k], partner)

    def xy_copy(k, d):
        i, peer = xy_peer(d)
        return remote(work.at[k, i], xybuf.at[k, d], xy_send.at[k, d], xy_recv.at[k, d], peer)

    def z_copy(k, d):
        part = zbuf.at[k, z]
        return remote(part, part, z_send.at[k, d], z_recv.at[k, d], z_peer(d))

    def xy_back(k, d):
        part = gout.at[32 * k + 16 * c + index]
        return remote(part, part, xy_send.at[2 + k, d], xy_recv.at[2 + k, d], xy_peer(d)[1])

    def core_back(k):
        part = gout.at[pl.ds(32 * k + 16 * c, 16)]
        return remote(part, part, core_send.at[2 + k], core_recv.at[2 + k], partner)

    row8 = lax.broadcasted_iota(jnp.int32, (8, SIDE), 0) + me * 8
    lane8 = lax.broadcasted_iota(jnp.int32, (8, SIDE), 1)

    def accumulate(slots):
        for ch in range(4):
            def add(d, acc):
                q = lax.rem(me + PEERS - d, PEERS)
                acc = list(acc)
                for j in slots:
                    a, block, shift = offset_of(offs, q, j)
                    piece = pltpu.roll(gin[j, d, ch * 8:ch * 8 + 8], shift, 1)
                    mine = jnp.where(row8 >= a, piece, 0.0)
                    other = piece - mine
                    target = jnp.where(lane8 < shift, block + 1, block)
                    for k in range(8):
                        mask = target == k
                        acc[k] = acc[k] + jnp.where(mask, mine, 0.0)
                        acc[8 + k] = acc[8 + k] + jnp.where(mask, other, 0.0)
                return tuple(acc)

            cols = [slice(k * SIDE, (k + 1) * SIDE) for k in range(8)]
            rows = slice(ch * 8, ch * 8 + 8)
            acc = [out[rows, s] for s in cols] + [nacc[rows, s] for s in cols]
            acc = lax.fori_loop(0, PEERS, add, tuple(acc))
            for k in range(8):
                out[rows, cols[k]] = acc[k]
                nacc[rows, cols[k]] = acc[8 + k]

    for k in range(2):
        core_copy(k).start()
    for k in range(2):
        core_copy(k).wait()
        work[k] = gprobe[pl.ds(32 * k + 16 * c, 16)] + cbuf[k]
        each_peer(lambda d: xy_copy(k, d).start())
    for k in range(2):
        each_peer(lambda d: xy_copy(k, d).wait())
        total = work[k, index]
        for d in range(1, PEERS):
            total = total + xybuf[k, d]
        zbuf[k, z] = total
        for d in range(1, 8):
            z_copy(k, d).start()
    for j in range(SLOTS - 1):
        each_peer(lambda d: object_copy(j, d).wait())
    accumulate(range(SLOTS - 1))
    each_peer(lambda d: object_copy(SLOTS - 1, d).wait())
    accumulate(range(SLOTS - 1, SLOTS))
    last_next = remote(nacc, nin, nxt_send.at[1], nxt_recv.at[1], at(me, above))
    last_next.start()
    for k in range(2):
        for d in range(1, 8):
            z_copy(k, d).wait()
        total = zbuf[k, 0]
        for d in range(1, 8):
            total = total + zbuf[k, d]
        gout[32 * k + 16 * c + index] = total
        each_peer(lambda d: xy_back(k, d).start())
    for k in range(2):
        each_peer(lambda d: xy_back(k, d).wait())
        core_back(k).start()
    last_next.wait()
    out[...] += nin[...]
    for k in range(2):
        core_back(k).wait()


def fused(offsets, cnt, shard, probe, pat, tab):
    vm = pl.BlockSpec(memory_space=pltpu.VMEM)
    sm = pl.BlockSpec(memory_space=pltpu.SMEM)
    hbm = pl.BlockSpec(memory_space=pltpu.HBM)
    dma = pltpu.SemaphoreType.DMA
    vmem = pltpu.VMEM
    return pl.pallas_call(
        fused_kernel,
        out_shape=[
            jax.ShapeDtypeStruct((32, 1024), f32),
            jax.ShapeDtypeStruct((64, 32, SIDE), f32),
        ],
        in_specs=[sm, sm, vm, hbm, hbm, hbm],
        out_specs=[vm, vm],
        scratch_shapes=[
            vmem((1, SIDE), jnp.int32),
            vmem((MODES, 2, SIDE, SIDE), f32),
            vmem((SLOTS, SIDE, SIDE), f32),
            vmem((4, 2, 256, 256), bf16),
            vmem((32, 1024), bf16),
            vmem((9, 32, SIDE), f32),
            vmem((9, 32, SIDE), f32),
            vmem((SLOTS, PEERS, 32, SIDE), bf16),
            vmem((SLOTS, PEERS, 32, SIDE), bf16),
            vmem((PEERS, 1, SIDE), jnp.int32),
            pltpu.SMEM((PEERS, 1, SIDE), jnp.int32),
            vmem((4, 256, SIDE), f32),
            vmem((4, SIDE, SIDE), f32),
            vmem((MODES, 2, SIDE, SIDE), f32),
            vmem((MODES, 2, SIDE, SIDE), f32),
            vmem((SIDE, SIDE), f32),
            vmem((64, 32, SIDE), f32),
            vmem((SLOTS, PEERS, 32, SIDE), f32),
            vmem((SLOTS, PEERS, 32, SIDE), f32),
            vmem((32, 1024), f32),
            vmem((32, 1024), f32),
            vmem((2, 16, 32, SIDE), f32),
            vmem((2, 16, 32, SIDE), f32),
            vmem((2, 16, 32, SIDE), f32),
            vmem((2, 8, 32, SIDE), f32),
            dma((4,)), dma((PEERS,)), dma((PEERS,)), dma((2,)), dma((2,)),
            dma((SLOTS, PEERS)), dma((SLOTS, PEERS)), dma((SLOTS, PEERS)), dma((SLOTS, PEERS)),
            dma((4,)), dma((4,)), dma((4, PEERS)), dma((4, PEERS)), dma((2, 8)), dma((2, 8)),
        ],
        compiler_params=pltpu.CompilerParams(
            collective_id=0, has_side_effects=True, vmem_limit_bytes=53 << 20
        ),
        name="ptychography",
    )(offsets, cnt, shard, probe, pat, tab)


def per_device(object_slices, probe_modes, offsets, counts, patterns):
    shard = object_slices.reshape(32, 1024)
    out, gout = fused(offsets.reshape(SLOTS, 2).T, counts, shard, probe_modes, patterns[0, 0], jnp.asarray(tables(SIDE)))
    return out.reshape(object_slices.shape), gout.reshape(probe_modes.shape)


def solution(mesh):
    placed = (
        P("tile", None, None, "pos", None),
        P(),
        P("tile", "pos", None, None),
        P("tile", "pos"),
        P("tile", "pos", None, None, None),
    )
    return jax.shard_map(
        per_device,
        mesh=mesh,
        in_specs=placed,
        out_specs=(P("tile", None, None, "pos", None), P()),
        check_vma=False,
    )
```

```python
import functools
import math

import jax
import jax.numpy as jnp
import ml_dtypes
import numpy as np
from jax import lax
from jax.experimental import pallas as pl
from jax.experimental.pallas import tpu as pltpu
from jax.sharding import PartitionSpec as P

f32 = jnp.float32
bf16 = jnp.bfloat16
MESH = pl.DeviceIdType.MESH
SIDE = 128
PEERS = 16
SLOTS = 4
TILES = 16
MODES = 8
CHUNKS = 2
UNIT = 64 // CHUNKS
PARTS = SIDE // UNIT


def signal_all(barrier, targets):
    for target in targets:
        pl.semaphore_signal(barrier, inc=1, device_id=target, device_id_type=MESH)
    pl.semaphore_wait(barrier, len(targets))


def remote(src, dst, send, recv, target):
    return pltpu.make_async_remote_copy(
        src_ref=src, dst_ref=dst, send_sem=send, recv_sem=recv,
        device_id=target, device_id_type=MESH,
    )


def at(pos, tile):
    return {"pos": pos, "tile": tile}


def offset_of(offs, q, j):
    a = offs[q, 0, 2 * j]
    b = offs[q, 0, 2 * j + 1]
    block = lax.div(b, SIDE)
    return a, block, b - block * SIDE


def tables(n):
    k=np.arange(n)
    f=np.exp(-2j*np.pi*(np.outer(k,k)%n)/n)/math.sqrt(n)
    fr=((k+n//2)%n-n//2)/n
    ph=np.exp(-1j*np.pi*24.0*fr**2)
    a=np.conj(f)@(ph[:,None]*f)
    out=[]
    for m in (a,f):
        right=np.block([[m.real,m.imag],[-m.imag,m.real]]).astype(np.float32)
        left=np.block([[m.real,-m.imag],[m.imag,m.real]]).astype(np.float32)
        for t in (right,left):
            hi=t.astype(ml_dtypes.bfloat16)
            lo=(t-hi.astype(np.float32)).astype(ml_dtypes.bfloat16)
            out.append(np.stack([hi,lo]))
    return np.stack(out)

def split(x):
    hi=x.astype(bf16)
    return hi,(x-hi.astype(f32)).astype(bf16)

def dot(a,b):
    return jnp.dot(a,b,preferred_element_type=f32)


def two_sided(tab, which, xr, xi):
    right_hi, right_lo = tab[2 * which, 0], tab[2 * which, 1]
    left_hi, left_lo = tab[2 * which + 1, 0], tab[2 * which + 1, 1]
    halves = []
    for m in range(0, MODES, 2):
        rows = [jnp.concatenate([xr[i], xi[i]], axis=1) for i in (m, m + 1)]
        hi, lo = split(jnp.concatenate(rows, axis=0))
        z = dot(hi, right_hi) + dot(lo, right_hi) + dot(hi, right_lo)
        top = jnp.concatenate([z[:SIDE, :SIDE], z[SIDE:, :SIDE]], axis=1)
        bottom = jnp.concatenate([z[:SIDE, SIDE:], z[SIDE:, SIDE:]], axis=1)
        halves.append(jnp.concatenate([top, bottom], axis=0))
    real, imag = [], []
    for half in halves:
        hi, lo = split(half)
        o = dot(left_hi, hi) + dot(left_hi, lo) + dot(left_lo, hi)
        real += [o[:SIDE, :SIDE], o[:SIDE, SIDE:]]
        imag += [o[SIDE:, :SIDE], o[SIDE:, SIDE:]]
    return real, imag


def fused_kernel(off_in, cnt, shard, probe_hbm, pat_hbm, tab_hbm, out, gout,
                 off, probe, pat, tab, nxt, own_f, nxt_f, wstage, pieces, offs_v, offs,
                 dbl, win, phi, psi, inten, gprobe, gp, gin, nacc, nin,
                 cbuf, work, xybuf, zbuf,
                 local_sem, off_send, off_recv, nxt_send, nxt_recv, win_send, win_recv,
                 obj_send, obj_recv, core_send, core_recv, xy_send, xy_recv, z_send, z_recv):
    me = lax.axis_index("pos")
    tile = lax.axis_index("tile")
    x, zl = lax.div(me, 4), lax.rem(me, 4)
    y, zh, c = lax.div(tile, 4), lax.rem(lax.div(tile, 2), 2), lax.rem(tile, 2)
    z = zh * 4 + zl
    index = y * 4 + x
    below = lax.rem(tile + TILES - 1, TILES)
    above = lax.rem(tile + 1, TILES)
    partner = at(me, tile + 1 - 2 * c)

    def xy_peer(d):
        px, py = lax.rem(x + lax.rem(d, 4), 4), lax.rem(y + lax.div(d, 4), 4)
        return py * 4 + px, at(px * 4 + zl, py * 4 + zh * 2 + c)

    def z_peer(d):
        pz = lax.rem(z + d, 8)
        return at(x * 4 + lax.rem(pz, 4), y * 4 + lax.div(pz, 4) * 2 + c)

    loads = [
        pltpu.make_async_copy(probe_hbm, probe, local_sem.at[0]),
        pltpu.make_async_copy(tab_hbm, tab, local_sem.at[1]),
        pltpu.make_async_copy(pat_hbm, pat, local_sem.at[2]),
    ]
    for load in loads:
        load.start()
    lane1 = lax.broadcasted_iota(jnp.int32, (1, SIDE), 1)
    row = jnp.zeros((1, SIDE), jnp.int32)
    for j in range(SLOTS):
        for i in range(2):
            row = jnp.where(lane1 == 2 * j + i, off_in[i, j], row)
    off[...] = row
    offs_v[me] = row
    targets = [at(lax.rem(me + d, PEERS), tile) for d in range(1, PEERS)]
    targets += [xy_peer(d)[1] for d in range(4, PEERS)]
    targets += [at(x * 4 + d, y * 4 + (1 - zh) * 2 + c) for d in range(4)]
    targets += [at(me, below), at(me, above), partner]
    signal_all(pltpu.get_barrier_semaphore(), targets)

    first_next = remote(shard, nxt, nxt_send.at[0], nxt_recv.at[0], at(me, below))
    first_next.start()

    def off_copy(d):
        return remote(off, offs_v.at[me], off_send.at[d], off_recv.at[d], at(lax.rem(me + d, PEERS), tile))

    def each_peer(action):
        def step(d, carry):
            action(d)
            return carry

        lax.fori_loop(1, PEERS, step, 0)

    each_peer(lambda d: off_copy(d).start())
    for block in range(8):
        own_f[block] = shard[:, block * SIDE:(block + 1) * SIDE].astype(f32)
    own_f[8] = jnp.zeros((32, SIDE), f32)
    nxt_f[8] = jnp.zeros((32, SIDE), f32)
    gprobe[...] = jnp.zeros(gprobe.shape, f32)
    out[...] = jnp.zeros(out.shape, f32)
    nacc[...] = jnp.zeros(nacc.shape, f32)
    each_peer(lambda d: off_copy(d).wait())
    to_smem = pltpu.make_async_copy(offs_v, offs, local_sem.at[3])
    to_smem.start()
    first_next.wait()
    for block in range(8):
        nxt_f[block] = nxt[:, block * SIDE:(block + 1) * SIDE].astype(f32)
    to_smem.wait()

    row32 = lax.rem(lax.broadcasted_iota(jnp.int32, (32, SIDE), 0), 8) + me * 8
    lane32 = lax.broadcasted_iota(jnp.int32, (32, SIDE), 1)

    def cut(q, j):
        a, block, shift = offset_of(offs, q, j)
        mask = row32 >= a
        left = jnp.where(mask, own_f[block], nxt_f[block])
        right = jnp.where(mask, own_f[block + 1], nxt_f[block + 1])
        return jnp.where(lane32 >= shift, left, right).astype(bf16)

    def window_copy(j, d):
        q = lax.rem(me + d, PEERS)
        return remote(wstage.at[j, q], pieces.at[j, me], win_send.at[j, d], win_recv.at[j, d], at(q, tile))

    def send_windows(j, carry):
        def send(d):
            q = lax.rem(me + d, PEERS)
            wstage[j, q] = cut(q, j)
            window_copy(j, d).start()

        each_peer(send)
        pieces[j, me] = cut(me, j)
        return carry

    lax.fori_loop(0, SLOTS, send_windows, 0)

    def object_copy(j, d):
        q = lax.rem(me + d, PEERS)
        return remote(gp.at[j, q], gin.at[j, d], obj_send.at[j, d], obj_recv.at[j, d], at(q, tile))

    for load in loads:
        load.wait()
    live_count = cnt[0, 0]

    def slot(j, carry):
        each_peer(lambda d: window_copy(j, d).wait())
        a, block, shift = offset_of(offs, me, j)
        for p in range(PEERS):
            piece = pieces[j, p].astype(f32)
            for ch in range(4):
                part = piece[ch * 8:ch * 8 + 8]
                dbl[ch, p * 8:p * 8 + 8] = part
                dbl[ch, SIDE + p * 8:SIDE + p * 8 + 8] = part
        for ch in range(4):
            win[ch] = pltpu.roll(dbl[ch, pl.ds(a, SIDE), :], lax.rem(SIDE - shift, SIDE), 1)
        w0r, w0i = win[0], win[1]
        xr, xi = [], []
        for m in range(MODES):
            pr, pi = probe[m, 0], probe[m, 1]
            xr.append(pr * w0r - pi * w0i)
            xi.append(pr * w0i + pi * w0r)
        zr, zi = two_sided(tab, 0, xr, xi)
        w1r, w1i = win[2], win[3]
        xr, xi = [], []
        for m in range(MODES):
            phi[m, 0] = zr[m]
            phi[m, 1] = zi[m]
            xr.append(zr[m] * w1r - zi[m] * w1i)
            xi.append(zr[m] * w1i + zi[m] * w1r)
        zr, zi = two_sided(tab, 1, xr, xi)
        total = -pat[j]
        for m in range(MODES):
            psi[m, 0] = zr[m]
            psi[m, 1] = zi[m]
            total = total + zr[m] * zr[m] + zi[m] * zi[m]
        slot_number = jnp.zeros((SIDE, SIDE), jnp.int32) + j
        inten[...] = jnp.where(slot_number < live_count, 2.0 * total, 0.0)

        res = inten[...]
        xr, xi = [], []
        for m in range(MODES):
            xr.append(psi[m, 0] * res)
            xi.append(psi[m, 1] * -res)
        zr, zi = two_sided(tab, 1, xr, xi)
        w1r, w1i = win[2], win[3]
        ar = ai = jnp.zeros((SIDE, SIDE), f32)
        xr, xi = [], []
        for m in range(MODES):
            fr, fi = phi[m, 0], phi[m, 1]
            ar = ar + (fr * zr[m] - fi * zi[m])
            ai = ai - (fr * zi[m] + fi * zr[m])
            xr.append(zr[m] * w1r - zi[m] * w1i)
            xi.append(zr[m] * w1i + zi[m] * w1r)
        for half in range(2):
            dbl[2, half * SIDE:(half + 1) * SIDE] = ar
            dbl[3, half * SIDE:(half + 1) * SIDE] = ai
        zr, zi = two_sided(tab, 0, xr, xi)
        w0r, w0i = win[0], win[1]
        ar = ai = jnp.zeros((SIDE, SIDE), f32)
        for m in range(MODES):
            pr, pi = probe[m, 0], probe[m, 1]
            ar = ar + (pr * zr[m] - pi * zi[m])
            ai = ai - (pr * zi[m] + pi * zr[m])
            gprobe[2 * m * PARTS:(2 * m + 1) * PARTS] += (zr[m] * w0r - zi[m] * w0i).reshape(PARTS, UNIT, SIDE)
            gprobe[(2 * m + 1) * PARTS:(2 * m + 2) * PARTS] -= (zr[m] * w0i + zi[m] * w0r).reshape(PARTS, UNIT, SIDE)
        for half in range(2):
            dbl[0, half * SIDE:(half + 1) * SIDE] = ar
            dbl[1, half * SIDE:(half + 1) * SIDE] = ai
        for ch in range(4):
            rolled = pltpu.roll(dbl[ch, pl.ds(SIDE - a, SIDE), :], shift, 1)
            for p in range(PEERS):
                gp[j, p, ch * 8:ch * 8 + 8] = rolled[p * 8:p * 8 + 8]
        each_peer(lambda d: object_copy(j, d).start())
        gin[j, 0] = gp[j, me]
        return carry

    lax.fori_loop(0, SLOTS, slot, 0)

    def core_copy(k):
        src = gprobe.at[pl.ds(32 * k + 16 * (1 - c), 16)]
        return remote(src, cbuf.at[k], core_send.at[k], core_recv.at[k], partner)

    def xy_copy(k, d):
        i, peer = xy_peer(d)
        return remote(work.at[k, i], xybuf.at[k, d], xy_send.at[k, d], xy_recv.at[k, d], peer)

    def z_copy(k, d):
        part = zbuf.at[k, z]
        return remote(part, part, z_send.at[k, d], z_recv.at[k, d], z_peer(d))

    def xy_back(k, d):
        part = gout.at[32 * k + 16 * c + index]
        return remote(part, part, xy_send.at[CHUNKS + k, d], xy_recv.at[CHUNKS + k, d], xy_peer(d)[1])

    def core_back(k):
        part = gout.at[pl.ds(32 * k + 16 * c, 16)]
        return remote(part, part, core_send.at[CHUNKS + k], core_recv.at[CHUNKS + k], partner)

    row8 = lax.broadcasted_iota(jnp.int32, (8, SIDE), 0) + me * 8
    lane8 = lax.broadcasted_iota(jnp.int32, (8, SIDE), 1)

    def accumulate(slots):
        group = 4
        for ch in range(4):
            def add(i, acc):
                acc = list(acc)
                for e in range(group):
                    d = i * group + e
                    q = lax.rem(me + PEERS - d, PEERS)
                    for j in slots:
                        a, block, shift = offset_of(offs, q, j)
                        piece = gin[j, d, ch * 8:ch * 8 + 8]
                        mine = jnp.where(row8 >= a, piece, 0.0)
                        other = piece - mine
                        target = jnp.where(lane8 < shift, block + 1, block)
                        for k in range(8):
                            mask = target == k
                            acc[k] = acc[k] + jnp.where(mask, mine, 0.0)
                            acc[8 + k] = acc[8 + k] + jnp.where(mask, other, 0.0)
                return tuple(acc)

            cols = [slice(k * SIDE, (k + 1) * SIDE) for k in range(8)]
            rows = slice(ch * 8, ch * 8 + 8)
            acc = [out[rows, s] for s in cols] + [nacc[rows, s] for s in cols]
            acc = lax.fori_loop(0, PEERS // group, add, tuple(acc))
            for k in range(8):
                out[rows, cols[k]] = acc[k]
                nacc[rows, cols[k]] = acc[8 + k]

    for k in range(CHUNKS):
        core_copy(k).start()
    for k in range(CHUNKS):
        core_copy(k).wait()
        work[k] = gprobe[pl.ds(32 * k + 16 * c, 16)] + cbuf[k]
        each_peer(lambda d: xy_copy(k, d).start())
    for k in range(CHUNKS):
        each_peer(lambda d: xy_copy(k, d).wait())
        total = work[k, index]
        for d in range(1, PEERS):
            total = total + xybuf[k, d]
        zbuf[k, z] = total
        for d in range(1, 8):
            z_copy(k, d).start()
    for j in range(SLOTS - 1):
        each_peer(lambda d: object_copy(j, d).wait())
    accumulate(range(SLOTS - 1))
    each_peer(lambda d: object_copy(SLOTS - 1, d).wait())
    accumulate(range(SLOTS - 1, SLOTS))
    last_next = remote(nacc, nin, nxt_send.at[1], nxt_recv.at[1], at(me, above))
    last_next.start()
    for k in range(CHUNKS):
        for d in range(1, 8):
            z_copy(k, d).wait()
        total = zbuf[k, 0]
        for d in range(1, 8):
            total = total + zbuf[k, d]
        gout[32 * k + 16 * c + index] = total
        each_peer(lambda d: xy_back(k, d).start())
    for k in range(CHUNKS):
        each_peer(lambda d: xy_back(k, d).wait())
        core_back(k).start()
    last_next.wait()
    out[...] += nin[...]
    for k in range(CHUNKS):
        core_back(k).wait()


def fused(offsets, cnt, shard, probe, pat, tab):
    vm = pl.BlockSpec(memory_space=pltpu.VMEM)
    sm = pl.BlockSpec(memory_space=pltpu.SMEM)
    hbm = pl.BlockSpec(memory_space=pltpu.HBM)
    dma = pltpu.SemaphoreType.DMA
    vmem = pltpu.VMEM
    return pl.pallas_call(
        fused_kernel,
        out_shape=[
            jax.ShapeDtypeStruct((32, 1024), f32),
            jax.ShapeDtypeStruct((32 * CHUNKS, UNIT, SIDE), f32),
        ],
        in_specs=[sm, sm, vm, hbm, hbm, hbm],
        out_specs=[vm, vm],
        scratch_shapes=[
            vmem((1, SIDE), jnp.int32),
            vmem((MODES, 2, SIDE, SIDE), f32),
            vmem((SLOTS, SIDE, SIDE), f32),
            vmem((4, 2, 256, 256), bf16),
            vmem((32, 1024), bf16),
            vmem((9, 32, SIDE), f32),
            vmem((9, 32, SIDE), f32),
            vmem((SLOTS, PEERS, 32, SIDE), bf16),
            vmem((SLOTS, PEERS, 32, SIDE), bf16),
            vmem((PEERS, 1, SIDE), jnp.int32),
            pltpu.SMEM((PEERS, 1, SIDE), jnp.int32),
            vmem((4, 256, SIDE), f32),
            vmem((4, SIDE, SIDE), f32),
            vmem((MODES, 2, SIDE, SIDE), f32),
            vmem((MODES, 2, SIDE, SIDE), f32),
            vmem((SIDE, SIDE), f32),
            vmem((32 * CHUNKS, UNIT, SIDE), f32),
            vmem((SLOTS, PEERS, 32, SIDE), f32),
            vmem((SLOTS, PEERS, 32, SIDE), f32),
            vmem((32, 1024), f32),
            vmem((32, 1024), f32),
            vmem((CHUNKS, 16, UNIT, SIDE), f32),
            vmem((CHUNKS, 16, UNIT, SIDE), f32),
            vmem((CHUNKS, 16, UNIT, SIDE), f32),
            vmem((CHUNKS, 8, UNIT, SIDE), f32),
            dma((4,)), dma((PEERS,)), dma((PEERS,)), dma((2,)), dma((2,)),
            dma((SLOTS, PEERS)), dma((SLOTS, PEERS)), dma((SLOTS, PEERS)), dma((SLOTS, PEERS)),
            dma((2 * CHUNKS,)), dma((2 * CHUNKS,)), dma((2 * CHUNKS, PEERS)), dma((2 * CHUNKS, PEERS)),
            dma((CHUNKS, 8)), dma((CHUNKS, 8)),
        ],
        compiler_params=pltpu.CompilerParams(
            collective_id=0, has_side_effects=True, vmem_limit_bytes=53 << 20
        ),
        name="ptychography",
    )(offsets, cnt, shard, probe, pat, tab)


def per_device(object_slices, probe_modes, offsets, counts, patterns):
    shard = object_slices.reshape(32, 1024)
    out, gout = fused(offsets.reshape(SLOTS, 2).T, counts, shard, probe_modes, patterns[0, 0], jnp.asarray(tables(SIDE)))
    return out.reshape(object_slices.shape), gout.reshape(probe_modes.shape)


def solution(mesh):
    placed = (
        P("tile", None, None, "pos", None),
        P(),
        P("tile", "pos", None, None),
        P("tile", "pos"),
        P("tile", "pos", None, None, None),
    )
    return jax.shard_map(
        per_device,
        mesh=mesh,
        in_specs=placed,
        out_specs=(P("tile", None, None, "pos", None), P()),
        check_vma=False,
    )
```

```python
import functools
import math

import jax
import jax.numpy as jnp
import ml_dtypes
import numpy as np
from jax import lax
from jax.experimental import pallas as pl
from jax.experimental.pallas import tpu as pltpu
from jax.sharding import PartitionSpec as P

f32 = jnp.float32
bf16 = jnp.bfloat16
MESH = pl.DeviceIdType.MESH
SIDE = 128
PEERS = 16
SLOTS = 4
TILES = 16
MODES = 8
HALF = 64
CHUNKS = 2
UNIT = 64 // CHUNKS
PARTS = SIDE // UNIT


def signal_all(barrier, targets):
    for target in targets:
        pl.semaphore_signal(barrier, inc=1, device_id=target, device_id_type=MESH)
    pl.semaphore_wait(barrier, len(targets))


def remote(src, dst, send, recv, target):
    return pltpu.make_async_remote_copy(
        src_ref=src, dst_ref=dst, send_sem=send, recv_sem=recv,
        device_id=target, device_id_type=MESH,
    )


def at(pos, tile):
    return {"pos": pos, "tile": tile}


def offset_of(offs, q, j):
    a = offs[q, 0, 2 * j]
    b = offs[q, 0, 2 * j + 1]
    block = lax.div(b, SIDE)
    return a, block, b - block * SIDE


def parts(t):
    hi = t.astype(np.float32).astype(ml_dtypes.bfloat16)
    return hi, (t.astype(np.float32) - hi.astype(np.float32)).astype(ml_dtypes.bfloat16)


def real_form(m):
    return np.block([[m.real, -m.imag], [m.imag, m.real]])


def tables(n):
    h = n // 2
    k = np.arange(n)
    f = np.exp(-2j * np.pi * (np.outer(k, k) % n) / n) / math.sqrt(n)
    fr = ((k + h) % n - h) / n
    a = np.conj(f) @ (np.exp(-1j * np.pi * 24.0 * fr ** 2)[:, None] * f)
    right = np.stack([np.stack(parts(real_form(m).T)) for m in (a, f)])
    pairs = [
        ((a[:h, :h] + a[:h, h:]) / 2, (a[:h, :h] - a[:h, h:]) / 2),
        (f[0::2, :h], f[1::2, :h]),
        (f[:h, 0::2], f[:h, 1::2]),
    ]
    left = []
    for pair in pairs:
        for m in pair:
            hi, lo = parts(real_form(m))
            left.append(np.block([[hi, hi], [lo, lo]]))
    return np.stack([*right[0], *right[1], *left])


def split(x):
    hi = x.astype(bf16)
    return hi, (x - hi.astype(f32)).astype(bf16)


def dot(a, b):
    return jnp.dot(a, b, preferred_element_type=f32)


def two_sided(tab, which, kind, xr, xi, before, after):
    right_hi, right_lo = tab[2 * which], tab[2 * which + 1]
    left_even, left_odd = tab[4 + 2 * kind], tab[5 + 2 * kind]
    fields = []
    for m in range(0, MODES, 2):
        rows = [jnp.concatenate([xr[i], xi[i]], axis=1) for i in (m, m + 1)]
        hi, lo = split(jnp.concatenate(rows, axis=0))
        fields.append(dot(hi, right_hi) + dot(lo, right_hi) + dot(hi, right_lo))
    real, imag = [], []
    for field in fields:
        quarter = [
            [
                jnp.concatenate(
                    [field[r:r + HALF, p:p + SIDE], field[SIDE + r:SIDE + r + HALF, p:p + SIDE]], axis=1
                )
                for r in (0, HALF)
            ]
            for p in (0, SIDE)
        ]
        if before:
            even = [first + second for first, second in quarter]
            odd = [first - second for first, second in quarter]
        else:
            even = [first for first, second in quarter]
            odd = [second for first, second in quarter]
        sums = []
        for table, value in ((left_even, even), (left_odd, odd)):
            hi, lo = split(jnp.concatenate(value, axis=0))
            o = dot(table, jnp.concatenate([hi, lo], axis=0))
            sums.append(o[:SIDE] + o[SIDE:])
        u, v = sums
        if after:
            u, v = u + v, u - v
        for m in (0, SIDE):
            real.append(jnp.concatenate([u[:HALF, m:m + SIDE], v[:HALF, m:m + SIDE]], axis=0))
            imag.append(jnp.concatenate([u[HALF:, m:m + SIDE], v[HALF:, m:m + SIDE]], axis=0))
    return real, imag


def fused_kernel(off_in, cnt, shard_hbm, probe_hbm, pat_hbm, tab_hbm, out, gout,
                 off, shard, probe, pat, tab, nxt, own_f, nxt_f, wstage, pieces, offs_v, offs,
                 dbl, win, phi, psi, inten, gprobe, gp, gin, nacc, nin,
                 cbuf, work, xybuf, zbuf,
                 local_sem, off_send, off_recv, nxt_send, nxt_recv, win_send, win_recv,
                 obj_send, obj_recv, core_send, core_recv, xy_send, xy_recv, z_send, z_recv):
    me = lax.axis_index("pos")
    tile = lax.axis_index("tile")
    x, zl = lax.div(me, 4), lax.rem(me, 4)
    y, zh, c = lax.div(tile, 4), lax.rem(lax.div(tile, 2), 2), lax.rem(tile, 2)
    z = zh * 4 + zl
    index = y * 4 + x
    below = lax.rem(tile + TILES - 1, TILES)
    above = lax.rem(tile + 1, TILES)
    partner = at(me, tile + 1 - 2 * c)

    def xy_peer(d):
        px, py = lax.rem(x + lax.rem(d, 4), 4), lax.rem(y + lax.div(d, 4), 4)
        return py * 4 + px, at(px * 4 + zl, py * 4 + zh * 2 + c)

    def z_peer(d):
        pz = lax.rem(z + d, 8)
        return at(x * 4 + lax.rem(pz, 4), y * 4 + lax.div(pz, 4) * 2 + c)

    shard_load = pltpu.make_async_copy(shard_hbm, shard, local_sem.at[4])
    shard_load.start()
    loads = [
        pltpu.make_async_copy(probe_hbm, probe, local_sem.at[0]),
        pltpu.make_async_copy(tab_hbm, tab, local_sem.at[1]),
        pltpu.make_async_copy(pat_hbm, pat, local_sem.at[2]),
    ]
    for load in loads:
        load.start()
    lane1 = lax.broadcasted_iota(jnp.int32, (1, SIDE), 1)
    row = jnp.zeros((1, SIDE), jnp.int32)
    for j in range(SLOTS):
        for i in range(2):
            row = jnp.where(lane1 == 2 * j + i, off_in[i, j], row)
    off[...] = row
    offs_v[me] = row
    targets = [at(lax.rem(me + d, PEERS), tile) for d in range(1, PEERS)]
    targets += [xy_peer(d)[1] for d in range(4, PEERS)]
    targets += [at(x * 4 + d, y * 4 + (1 - zh) * 2 + c) for d in range(4)]
    targets += [at(me, below), at(me, above), partner]
    signal_all(pltpu.get_barrier_semaphore(), targets)

    shard_load.wait()
    first_next = remote(shard, nxt, nxt_send.at[0], nxt_recv.at[0], at(me, below))
    first_next.start()

    def off_copy(d):
        return remote(off, offs_v.at[me], off_send.at[d], off_recv.at[d], at(lax.rem(me + d, PEERS), tile))

    def each_peer(action):
        def step(d, carry):
            action(d)
            return carry

        lax.fori_loop(1, PEERS, step, 0)

    each_peer(lambda d: off_copy(d).start())
    for block in range(8):
        own_f[block] = shard[:, block * SIDE:(block + 1) * SIDE].astype(f32)
    own_f[8] = jnp.zeros((32, SIDE), f32)
    nxt_f[8] = jnp.zeros((32, SIDE), f32)
    gprobe[...] = jnp.zeros(gprobe.shape, f32)
    out[...] = jnp.zeros(out.shape, f32)
    nacc[...] = jnp.zeros(nacc.shape, f32)
    each_peer(lambda d: off_copy(d).wait())
    to_smem = pltpu.make_async_copy(offs_v, offs, local_sem.at[3])
    to_smem.start()
    first_next.wait()
    for block in range(8):
        nxt_f[block] = nxt[:, block * SIDE:(block + 1) * SIDE].astype(f32)
    to_smem.wait()

    row32 = lax.rem(lax.broadcasted_iota(jnp.int32, (32, SIDE), 0), 8) + me * 8
    lane32 = lax.broadcasted_iota(jnp.int32, (32, SIDE), 1)

    def cut(q, j):
        a, block, shift = offset_of(offs, q, j)
        mask = row32 >= a
        left = jnp.where(mask, own_f[block], nxt_f[block])
        right = jnp.where(mask, own_f[block + 1], nxt_f[block + 1])
        return jnp.where(lane32 >= shift, left, right).astype(bf16)

    def window_copy(j, d):
        q = lax.rem(me + d, PEERS)
        return remote(wstage.at[j, q], pieces.at[j, me], win_send.at[j, d], win_recv.at[j, d], at(q, tile))

    def send_windows(j, carry):
        def send(d):
            q = lax.rem(me + d, PEERS)
            wstage[j, q] = cut(q, j)
            window_copy(j, d).start()

        each_peer(send)
        pieces[j, me] = cut(me, j)
        return carry

    lax.fori_loop(0, SLOTS, send_windows, 0)

    def object_copy(j, d):
        q = lax.rem(me + d, PEERS)
        return remote(gp.at[j, q], gin.at[j, d], obj_send.at[j, d], obj_recv.at[j, d], at(q, tile))

    for load in loads:
        load.wait()
    live_count = cnt[0, 0]

    def slot(j, carry):
        each_peer(lambda d: window_copy(j, d).wait())
        a, block, shift = offset_of(offs, me, j)
        for p in range(PEERS):
            piece = pieces[j, p].astype(f32)
            for ch in range(4):
                part = piece[ch * 8:ch * 8 + 8]
                dbl[ch, p * 8:p * 8 + 8] = part
                dbl[ch, SIDE + p * 8:SIDE + p * 8 + 8] = part
        for ch in range(4):
            win[ch] = pltpu.roll(dbl[ch, pl.ds(a, SIDE), :], lax.rem(SIDE - shift, SIDE), 1)
        w0r, w0i = win[0], win[1]
        xr, xi = [], []
        for m in range(MODES):
            pr, pi = probe[m, 0], probe[m, 1]
            xr.append(pr * w0r - pi * w0i)
            xi.append(pr * w0i + pi * w0r)
        zr, zi = two_sided(tab, 0, 0, xr, xi, True, True)
        w1r, w1i = win[2], win[3]
        xr, xi = [], []
        for m in range(MODES):
            phi[m, 0] = zr[m]
            phi[m, 1] = zi[m]
            xr.append(zr[m] * w1r - zi[m] * w1i)
            xi.append(zr[m] * w1i + zi[m] * w1r)
        zr, zi = two_sided(tab, 1, 1, xr, xi, True, False)
        measured = [pat[j, pl.ds(first, HALF, stride=2), :] for first in range(2)]
        total = -jnp.concatenate(measured, axis=0)
        for m in range(MODES):
            psi[m, 0] = zr[m]
            psi[m, 1] = zi[m]
            total = total + zr[m] * zr[m] + zi[m] * zi[m]
        slot_number = jnp.zeros((SIDE, SIDE), jnp.int32) + j
        inten[...] = jnp.where(slot_number < live_count, 2.0 * total, 0.0)

        res = inten[...]
        xr, xi = [], []
        for m in range(MODES):
            xr.append(psi[m, 0] * res)
            xi.append(psi[m, 1] * -res)
        zr, zi = two_sided(tab, 1, 2, xr, xi, False, True)
        w1r, w1i = win[2], win[3]
        ar = ai = jnp.zeros((SIDE, SIDE), f32)
        xr, xi = [], []
        for m in range(MODES):
            fr, fi = phi[m, 0], phi[m, 1]
            ar = ar + (fr * zr[m] - fi * zi[m])
            ai = ai - (fr * zi[m] + fi * zr[m])
            xr.append(zr[m] * w1r - zi[m] * w1i)
            xi.append(zr[m] * w1i + zi[m] * w1r)
        for half in range(2):
            dbl[2, half * SIDE:(half + 1) * SIDE] = ar
            dbl[3, half * SIDE:(half + 1) * SIDE] = ai
        zr, zi = two_sided(tab, 0, 0, xr, xi, True, True)
        w0r, w0i = win[0], win[1]
        ar = ai = jnp.zeros((SIDE, SIDE), f32)
        for m in range(MODES):
            pr, pi = probe[m, 0], probe[m, 1]
            ar = ar + (pr * zr[m] - pi * zi[m])
            ai = ai - (pr * zi[m] + pi * zr[m])
            gprobe[2 * m * PARTS:(2 * m + 1) * PARTS] += (zr[m] * w0r - zi[m] * w0i).reshape(PARTS, UNIT, SIDE)
            gprobe[(2 * m + 1) * PARTS:(2 * m + 2) * PARTS] -= (zr[m] * w0i + zi[m] * w0r).reshape(PARTS, UNIT, SIDE)
        for half in range(2):
            dbl[0, half * SIDE:(half + 1) * SIDE] = ar
            dbl[1, half * SIDE:(half + 1) * SIDE] = ai
        for ch in range(4):
            rolled = pltpu.roll(dbl[ch, pl.ds(SIDE - a, SIDE), :], shift, 1)
            for p in range(PEERS):
                gp[j, p, ch * 8:ch * 8 + 8] = rolled[p * 8:p * 8 + 8]
        each_peer(lambda d: object_copy(j, d).start())
        gin[j, 0] = gp[j, me]
        return carry

    lax.fori_loop(0, SLOTS, slot, 0)

    def core_copy(k):
        src = gprobe.at[pl.ds(32 * k + 16 * (1 - c), 16)]
        return remote(src, cbuf.at[k], core_send.at[k], core_recv.at[k], partner)

    def xy_copy(k, d):
        i, peer = xy_peer(d)
        return remote(work.at[k, i], xybuf.at[k, d], xy_send.at[k, d], xy_recv.at[k, d], peer)

    def z_copy(k, d):
        part = zbuf.at[k, z]
        return remote(part, part, z_send.at[k, d], z_recv.at[k, d], z_peer(d))

    def xy_back(k, d):
        part = gout.at[32 * k + 16 * c + index]
        return remote(part, part, xy_send.at[CHUNKS + k, d], xy_recv.at[CHUNKS + k, d], xy_peer(d)[1])

    def core_back(k):
        part = gout.at[pl.ds(32 * k + 16 * c, 16)]
        return remote(part, part, core_send.at[CHUNKS + k], core_recv.at[CHUNKS + k], partner)

    row8 = lax.broadcasted_iota(jnp.int32, (8, SIDE), 0) + me * 8
    lane8 = lax.broadcasted_iota(jnp.int32, (8, SIDE), 1)

    def accumulate(slots):
        group = 4
        for ch in range(4):
            def add(i, acc):
                acc = list(acc)
                for e in range(group):
                    d = i * group + e
                    q = lax.rem(me + PEERS - d, PEERS)
                    for j in slots:
                        a, block, shift = offset_of(offs, q, j)
                        piece = gin[j, d, ch * 8:ch * 8 + 8]
                        mine = jnp.where(row8 >= a, piece, 0.0)
                        other = piece - mine
                        target = jnp.where(lane8 < shift, block + 1, block)
                        for k in range(8):
                            mask = target == k
                            acc[k] = acc[k] + jnp.where(mask, mine, 0.0)
                            acc[8 + k] = acc[8 + k] + jnp.where(mask, other, 0.0)
                return tuple(acc)

            cols = [slice(k * SIDE, (k + 1) * SIDE) for k in range(8)]
            rows = slice(ch * 8, ch * 8 + 8)
            acc = [out[rows, s] for s in cols] + [nacc[rows, s] for s in cols]
            acc = lax.fori_loop(0, PEERS // group, add, tuple(acc))
            for k in range(8):
                out[rows, cols[k]] = acc[k]
                nacc[rows, cols[k]] = acc[8 + k]

    for k in range(CHUNKS):
        core_copy(k).start()
    for k in range(CHUNKS):
        core_copy(k).wait()
        work[k] = gprobe[pl.ds(32 * k + 16 * c, 16)] + cbuf[k]
        each_peer(lambda d: xy_copy(k, d).start())
    for j in range(SLOTS - 1):
        each_peer(lambda d: object_copy(j, d).wait())
    accumulate(range(SLOTS - 1))
    for k in range(CHUNKS):
        each_peer(lambda d: xy_copy(k, d).wait())
        total = work[k, index]
        for d in range(1, PEERS):
            total = total + xybuf[k, d]
        zbuf[k, z] = total
        for d in range(1, 8):
            z_copy(k, d).start()
    each_peer(lambda d: object_copy(SLOTS - 1, d).wait())
    accumulate(range(SLOTS - 1, SLOTS))
    last_next = remote(nacc, nin, nxt_send.at[1], nxt_recv.at[1], at(me, above))
    last_next.start()
    for k in range(CHUNKS):
        for d in range(1, 8):
            z_copy(k, d).wait()
        total = zbuf[k, 0]
        for d in range(1, 8):
            total = total + zbuf[k, d]
        gout[32 * k + 16 * c + index] = total
        each_peer(lambda d: xy_back(k, d).start())
    for k in range(CHUNKS):
        each_peer(lambda d: xy_back(k, d).wait())
        core_back(k).start()
    last_next.wait()
    out[...] += nin[...]
    for k in range(CHUNKS):
        core_back(k).wait()


def fused(offsets, cnt, shard, probe, pat, tab):
    vm = pl.BlockSpec(memory_space=pltpu.VMEM)
    sm = pl.BlockSpec(memory_space=pltpu.SMEM)
    hbm = pl.BlockSpec(memory_space=pltpu.HBM)
    dma = pltpu.SemaphoreType.DMA
    vmem = pltpu.VMEM
    return pl.pallas_call(
        fused_kernel,
        out_shape=[
            jax.ShapeDtypeStruct((32, 1024), f32),
            jax.ShapeDtypeStruct((32 * CHUNKS, UNIT, SIDE), f32),
        ],
        in_specs=[sm, sm, hbm, hbm, hbm, hbm],
        out_specs=[vm, vm],
        scratch_shapes=[
            vmem((1, SIDE), jnp.int32),
            vmem((32, 1024), bf16),
            vmem((MODES, 2, SIDE, SIDE), f32),
            vmem((SLOTS, SIDE, SIDE), f32),
            vmem((10, 256, 256), bf16),
            vmem((32, 1024), bf16),
            vmem((9, 32, SIDE), f32),
            vmem((9, 32, SIDE), f32),
            vmem((SLOTS, PEERS, 32, SIDE), bf16),
            vmem((SLOTS, PEERS, 32, SIDE), bf16),
            vmem((PEERS, 1, SIDE), jnp.int32),
            pltpu.SMEM((PEERS, 1, SIDE), jnp.int32),
            vmem((4, 256, SIDE), f32),
            vmem((4, SIDE, SIDE), f32),
            vmem((MODES, 2, SIDE, SIDE), f32),
            vmem((MODES, 2, SIDE, SIDE), f32),
            vmem((SIDE, SIDE), f32),
            vmem((32 * CHUNKS, UNIT, SIDE), f32),
            vmem((SLOTS, PEERS, 32, SIDE), f32),
            vmem((SLOTS, PEERS, 32, SIDE), f32),
            vmem((32, 1024), f32),
            vmem((32, 1024), f32),
            vmem((CHUNKS, 16, UNIT, SIDE), f32),
            vmem((CHUNKS, 16, UNIT, SIDE), f32),
            vmem((CHUNKS, 16, UNIT, SIDE), f32),
            vmem((CHUNKS, 8, UNIT, SIDE), f32),
            dma((5,)), dma((PEERS,)), dma((PEERS,)), dma((2,)), dma((2,)),
            dma((SLOTS, PEERS)), dma((SLOTS, PEERS)), dma((SLOTS, PEERS)), dma((SLOTS, PEERS)),
            dma((2 * CHUNKS,)), dma((2 * CHUNKS,)), dma((2 * CHUNKS, PEERS)), dma((2 * CHUNKS, PEERS)),
            dma((CHUNKS, 8)), dma((CHUNKS, 8)),
        ],
        compiler_params=pltpu.CompilerParams(
            collective_id=0, has_side_effects=True, vmem_limit_bytes=40 << 20
        ),
        name="ptychography",
    )(offsets, cnt, *[pltpu.with_memory_space_constraint(v, pltpu.HBM) for v in (shard, probe, pat, tab)])


def per_device(object_slices, probe_modes, offsets, counts, patterns):
    shard = object_slices.reshape(32, 1024)
    out, gout = fused(offsets.reshape(SLOTS, 2).T, counts, shard, probe_modes, patterns[0, 0], jnp.asarray(tables(SIDE)))
    return out.reshape(object_slices.shape), gout.reshape(probe_modes.shape)


def solution(mesh):
    placed = (
        P("tile", None, None, "pos", None),
        P(),
        P("tile", "pos", None, None),
        P("tile", "pos"),
        P("tile", "pos", None, None, None),
    )
    return jax.shard_map(
        per_device,
        mesh=mesh,
        in_specs=placed,
        out_specs=(P("tile", None, None, "pos", None), P()),
        check_vma=False,
    )
```

```python
import functools
import math

import jax
import jax.numpy as jnp
import ml_dtypes
import numpy as np
from jax import lax
from jax.experimental import pallas as pl
from jax.experimental.pallas import tpu as pltpu
from jax.sharding import PartitionSpec as P

f32 = jnp.float32
bf16 = jnp.bfloat16
MESH = pl.DeviceIdType.MESH
SIDE = 128
PEERS = 16
SLOTS = 4
TILES = 16
MODES = 8
HALF = 64
CHUNKS = 2
UNIT = 64 // CHUNKS
PARTS = SIDE // UNIT


def signal_all(barrier, targets):
    for target in targets:
        pl.semaphore_signal(barrier, inc=1, device_id=target, device_id_type=MESH)
    pl.semaphore_wait(barrier, len(targets))


def remote(src, dst, send, recv, target):
    return pltpu.make_async_remote_copy(
        src_ref=src, dst_ref=dst, send_sem=send, recv_sem=recv,
        device_id=target, device_id_type=MESH,
    )


def at(pos, tile):
    return {"pos": pos, "tile": tile}


def offset_of(offs, q, j):
    a = offs[q, 0, 2 * j]
    b = offs[q, 0, 2 * j + 1]
    block = lax.div(b, SIDE)
    return a, block, b - block * SIDE


def parts(t):
    hi = t.astype(np.float32).astype(ml_dtypes.bfloat16)
    return hi, (t.astype(np.float32) - hi.astype(np.float32)).astype(ml_dtypes.bfloat16)


def real_form(m):
    return np.block([[m.real, -m.imag], [m.imag, m.real]])


def tables(n):
    h = n // 2
    k = np.arange(n)
    f = np.exp(-2j * np.pi * (np.outer(k, k) % n) / n) / math.sqrt(n)
    fr = ((k + h) % n - h) / n
    a = np.conj(f) @ (np.exp(-1j * np.pi * 24.0 * fr ** 2)[:, None] * f)
    right = np.stack([np.stack(parts(real_form(m).T)) for m in (a, f)])
    pairs = [
        ((a[:h, :h] + a[:h, h:]) / 2, (a[:h, :h] - a[:h, h:]) / 2),
        (f[0::2, :h], f[1::2, :h]),
        (f[:h, 0::2], f[:h, 1::2]),
    ]
    left = []
    for pair in pairs:
        for m in pair:
            hi, lo = parts(real_form(m))
            left.append(np.block([[hi, hi], [lo, lo]]))
    return np.stack([*right[0], *right[1], *left])


def split(x):
    hi = x.astype(bf16)
    return hi, (x - hi.astype(f32)).astype(bf16)


def dot(a, b):
    return jnp.dot(a, b, preferred_element_type=f32)


def two_sided(tab, which, kind, xr, xi, before, after):
    right_hi, right_lo = tab[2 * which], tab[2 * which + 1]
    left_even, left_odd = tab[4 + 2 * kind], tab[5 + 2 * kind]
    fields = []
    for m in range(0, MODES, 2):
        rows = [jnp.concatenate([xr[i], xi[i]], axis=1) for i in (m, m + 1)]
        hi, lo = split(jnp.concatenate(rows, axis=0))
        fields.append(dot(hi, right_hi) + dot(lo, right_hi) + dot(hi, right_lo))
    real, imag = [], []
    for field in fields:
        quarter = [
            [
                jnp.concatenate(
                    [field[r:r + HALF, p:p + SIDE], field[SIDE + r:SIDE + r + HALF, p:p + SIDE]], axis=1
                )
                for r in (0, HALF)
            ]
            for p in (0, SIDE)
        ]
        if before:
            even = [first + second for first, second in quarter]
            odd = [first - second for first, second in quarter]
        else:
            even = [first for first, second in quarter]
            odd = [second for first, second in quarter]
        sums = []
        for table, value in ((left_even, even), (left_odd, odd)):
            hi, lo = split(jnp.concatenate(value, axis=0))
            o = dot(table, jnp.concatenate([hi, lo], axis=0))
            sums.append(o[:SIDE] + o[SIDE:])
        u, v = sums
        if after:
            u, v = u + v, u - v
        for m in (0, SIDE):
            real.append(jnp.concatenate([u[:HALF, m:m + SIDE], v[:HALF, m:m + SIDE]], axis=0))
            imag.append(jnp.concatenate([u[HALF:, m:m + SIDE], v[HALF:, m:m + SIDE]], axis=0))
    return real, imag


def fused_kernel(off_in, cnt, shard_hbm, probe_hbm, pat_hbm, tab_hbm, out, gout,
                 off, shard, probe, pat, tab, nxt, own_f, nxt_f, wstage, pieces, offs_v, offs,
                 dbl, win, phi, psi, inten, gprobe, gp, gin, nacc, nin,
                 cbuf, work, xybuf, zbuf,
                 local_sem, off_send, off_recv, nxt_send, nxt_recv, win_send, win_recv,
                 obj_send, obj_recv, core_send, core_recv, xy_send, xy_recv, z_send, z_recv):
    me = lax.axis_index("pos")
    tile = lax.axis_index("tile")
    x, zl = lax.div(me, 4), lax.rem(me, 4)
    y, zh, c = lax.div(tile, 4), lax.rem(lax.div(tile, 2), 2), lax.rem(tile, 2)
    z = zh * 4 + zl
    index = y * 4 + x
    below = lax.rem(tile + TILES - 1, TILES)
    above = lax.rem(tile + 1, TILES)
    partner = at(me, tile + 1 - 2 * c)

    def xy_peer(d):
        px, py = lax.rem(x + lax.rem(d, 4), 4), lax.rem(y + lax.div(d, 4), 4)
        return py * 4 + px, at(px * 4 + zl, py * 4 + zh * 2 + c)

    def z_peer(d):
        pz = lax.rem(z + d, 8)
        return at(x * 4 + lax.rem(pz, 4), y * 4 + lax.div(pz, 4) * 2 + c)

    shard_load = pltpu.make_async_copy(shard_hbm, shard, local_sem.at[4])
    shard_load.start()
    loads = [
        pltpu.make_async_copy(probe_hbm, probe, local_sem.at[0]),
        pltpu.make_async_copy(tab_hbm, tab, local_sem.at[1]),
        pltpu.make_async_copy(pat_hbm, pat, local_sem.at[2]),
    ]
    for load in loads:
        load.start()
    lane1 = lax.broadcasted_iota(jnp.int32, (1, SIDE), 1)
    row = jnp.zeros((1, SIDE), jnp.int32)
    for j in range(SLOTS):
        for i in range(2):
            row = jnp.where(lane1 == 2 * j + i, off_in[i, j], row)
    off[...] = row
    offs_v[me] = row
    targets = [at(lax.rem(me + d, PEERS), tile) for d in range(1, PEERS)]
    targets += [xy_peer(d)[1] for d in range(4, PEERS)]
    targets += [at(x * 4 + d, y * 4 + (1 - zh) * 2 + c) for d in range(4)]
    targets += [at(me, below), at(me, above), partner]
    signal_all(pltpu.get_barrier_semaphore(), targets)

    shard_load.wait()
    first_next = remote(shard, nxt, nxt_send.at[0], nxt_recv.at[0], at(me, below))
    first_next.start()

    def off_copy(d):
        return remote(off, offs_v.at[me], off_send.at[d], off_recv.at[d], at(lax.rem(me + d, PEERS), tile))

    def each_peer(action):
        def step(d, carry):
            action(d)
            return carry

        lax.fori_loop(1, PEERS, step, 0)

    each_peer(lambda d: off_copy(d).start())
    for block in range(8):
        own_f[block] = shard[:, block * SIDE:(block + 1) * SIDE].astype(f32)
    own_f[8] = jnp.zeros((32, SIDE), f32)
    nxt_f[8] = jnp.zeros((32, SIDE), f32)
    gprobe[...] = jnp.zeros(gprobe.shape, f32)
    out[...] = jnp.zeros(out.shape, f32)
    nacc[...] = jnp.zeros(nacc.shape, f32)
    each_peer(lambda d: off_copy(d).wait())
    to_smem = pltpu.make_async_copy(offs_v, offs, local_sem.at[3])
    to_smem.start()
    first_next.wait()
    for block in range(8):
        nxt_f[block] = nxt[:, block * SIDE:(block + 1) * SIDE].astype(f32)
    to_smem.wait()

    row32 = lax.rem(lax.broadcasted_iota(jnp.int32, (32, SIDE), 0), 8) + me * 8
    lane32 = lax.broadcasted_iota(jnp.int32, (32, SIDE), 1)

    def cut(q, j):
        a, block, shift = offset_of(offs, q, j)
        mask = row32 >= a
        left = jnp.where(mask, own_f[block], nxt_f[block])
        right = jnp.where(mask, own_f[block + 1], nxt_f[block + 1])
        return jnp.where(lane32 >= shift, left, right).astype(bf16)

    def window_copy(j, d):
        q = lax.rem(me + d, PEERS)
        return remote(wstage.at[j, q], pieces.at[j, me], win_send.at[j, d], win_recv.at[j, d], at(q, tile))

    def send_windows(j, carry):
        def send(d):
            q = lax.rem(me + d, PEERS)
            wstage[j, q] = cut(q, j)
            window_copy(j, d).start()

        each_peer(send)
        pieces[j, me] = cut(me, j)
        return carry

    lax.fori_loop(0, SLOTS, send_windows, 0)

    def object_copy(j, d):
        q = lax.rem(me + d, PEERS)
        return remote(gp.at[j, q], gin.at[j, d], obj_send.at[j, d], obj_recv.at[j, d], at(q, tile))

    for load in loads:
        load.wait()
    live_count = cnt[0, 0]

    def slot(j, carry):
        each_peer(lambda d: window_copy(j, d).wait())
        a, block, shift = offset_of(offs, me, j)
        for p in range(PEERS):
            piece = pieces[j, p].astype(f32)
            for ch in range(4):
                part = piece[ch * 8:ch * 8 + 8]
                dbl[ch, p * 8:p * 8 + 8] = part
                dbl[ch, SIDE + p * 8:SIDE + p * 8 + 8] = part
        for ch in range(4):
            win[ch] = pltpu.roll(dbl[ch, pl.ds(a, SIDE), :], lax.rem(SIDE - shift, SIDE), 1)
        w0r, w0i = win[0], win[1]
        xr, xi = [], []
        for m in range(MODES):
            pr, pi = probe[m, 0], probe[m, 1]
            xr.append(pr * w0r - pi * w0i)
            xi.append(pr * w0i + pi * w0r)
        zr, zi = two_sided(tab, 0, 0, xr, xi, True, True)
        w1r, w1i = win[2], win[3]
        xr, xi = [], []
        for m in range(MODES):
            phi[m, 0] = zr[m]
            phi[m, 1] = zi[m]
            xr.append(zr[m] * w1r - zi[m] * w1i)
            xi.append(zr[m] * w1i + zi[m] * w1r)
        zr, zi = two_sided(tab, 1, 1, xr, xi, True, False)
        measured = [pat[j, pl.ds(first, HALF, stride=2), :] for first in range(2)]
        total = -jnp.concatenate(measured, axis=0)
        for m in range(MODES):
            psi[m, 0] = zr[m]
            psi[m, 1] = zi[m]
            total = total + zr[m] * zr[m] + zi[m] * zi[m]
        slot_number = jnp.zeros((SIDE, SIDE), jnp.int32) + j
        inten[...] = jnp.where(slot_number < live_count, 2.0 * total, 0.0)

        res = inten[...]
        xr, xi = [], []
        for m in range(MODES):
            xr.append(psi[m, 0] * res)
            xi.append(psi[m, 1] * -res)
        zr, zi = two_sided(tab, 1, 2, xr, xi, False, True)
        w1r, w1i = win[2], win[3]
        ar = ai = jnp.zeros((SIDE, SIDE), f32)
        xr, xi = [], []
        for m in range(MODES):
            fr, fi = phi[m, 0], phi[m, 1]
            ar = ar + (fr * zr[m] - fi * zi[m])
            ai = ai - (fr * zi[m] + fi * zr[m])
            xr.append(zr[m] * w1r - zi[m] * w1i)
            xi.append(zr[m] * w1i + zi[m] * w1r)
        for half in range(2):
            dbl[2, half * SIDE:(half + 1) * SIDE] = ar
            dbl[3, half * SIDE:(half + 1) * SIDE] = ai
        zr, zi = two_sided(tab, 0, 0, xr, xi, True, True)
        w0r, w0i = win[0], win[1]
        ar = ai = jnp.zeros((SIDE, SIDE), f32)
        for m in range(MODES):
            pr, pi = probe[m, 0], probe[m, 1]
            ar = ar + (pr * zr[m] - pi * zi[m])
            ai = ai - (pr * zi[m] + pi * zr[m])
            gprobe[2 * m * PARTS:(2 * m + 1) * PARTS] += (zr[m] * w0r - zi[m] * w0i).reshape(PARTS, UNIT, SIDE)
            gprobe[(2 * m + 1) * PARTS:(2 * m + 2) * PARTS] -= (zr[m] * w0i + zi[m] * w0r).reshape(PARTS, UNIT, SIDE)
        for half in range(2):
            dbl[0, half * SIDE:(half + 1) * SIDE] = ar
            dbl[1, half * SIDE:(half + 1) * SIDE] = ai
        for ch in range(4):
            rolled = pltpu.roll(dbl[ch, pl.ds(SIDE - a, SIDE), :], shift, 1)
            for p in range(PEERS):
                gp[j, p, ch * 8:ch * 8 + 8] = rolled[p * 8:p * 8 + 8]
        each_peer(lambda d: object_copy(j, d).start())
        gin[j, 0] = gp[j, me]
        return carry

    lax.fori_loop(0, SLOTS, slot, 0)

    def core_copy(k):
        src = gprobe.at[pl.ds(32 * k + 16 * (1 - c), 16)]
        return remote(src, cbuf.at[k], core_send.at[k], core_recv.at[k], partner)

    def xy_copy(k, d):
        i, peer = xy_peer(d)
        return remote(work.at[k, i], xybuf.at[k, d], xy_send.at[k, d], xy_recv.at[k, d], peer)

    def z_copy(k, d):
        part = zbuf.at[k, z]
        return remote(part, part, z_send.at[k, d], z_recv.at[k, d], z_peer(d))

    def xy_back(k, d):
        part = gout.at[32 * k + 16 * c + index]
        return remote(part, part, xy_send.at[CHUNKS + k, d], xy_recv.at[CHUNKS + k, d], xy_peer(d)[1])

    def core_back(k):
        part = gout.at[pl.ds(32 * k + 16 * c, 16)]
        return remote(part, part, core_send.at[CHUNKS + k], core_recv.at[CHUNKS + k], partner)

    row8 = lax.broadcasted_iota(jnp.int32, (8, SIDE), 0) + me * 8
    lane8 = lax.broadcasted_iota(jnp.int32, (8, SIDE), 1)

    def accumulate(slots):
        group = 4
        for ch in range(4):
            def add(i, acc):
                acc = list(acc)
                for e in range(group):
                    d = i * group + e
                    q = lax.rem(me + PEERS - d, PEERS)
                    for j in slots:
                        a, block, shift = offset_of(offs, q, j)
                        piece = gin[j, d, ch * 8:ch * 8 + 8]
                        mine = jnp.where(row8 >= a, piece, 0.0)
                        other = piece - mine
                        target = jnp.where(lane8 < shift, block + 1, block)
                        for k in range(8):
                            mask = target == k
                            acc[k] = acc[k] + jnp.where(mask, mine, 0.0)
                            acc[8 + k] = acc[8 + k] + jnp.where(mask, other, 0.0)
                return tuple(acc)

            cols = [slice(k * SIDE, (k + 1) * SIDE) for k in range(8)]
            rows = slice(ch * 8, ch * 8 + 8)
            acc = [out[rows, s] for s in cols] + [nacc[rows, s] for s in cols]
            acc = lax.fori_loop(0, PEERS // group, add, tuple(acc))
            for k in range(8):
                out[rows, cols[k]] = acc[k]
                nacc[rows, cols[k]] = acc[8 + k]

    for k in range(CHUNKS):
        core_copy(k).start()
    for k in range(CHUNKS):
        core_copy(k).wait()
        work[k] = gprobe[pl.ds(32 * k + 16 * c, 16)] + cbuf[k]
        each_peer(lambda d: xy_copy(k, d).start())
    for j in range(SLOTS - 1):
        each_peer(lambda d: object_copy(j, d).wait())
    accumulate(range(SLOTS - 1))
    for k in range(CHUNKS):
        each_peer(lambda d: xy_copy(k, d).wait())
        total = work[k, index]
        for d in range(1, PEERS):
            total = total + xybuf[k, d]
        zbuf[k, z] = total
        for d in range(1, 8):
            z_copy(k, d).start()
    each_peer(lambda d: object_copy(SLOTS - 1, d).wait())
    accumulate(range(SLOTS - 1, SLOTS))
    last_next = remote(nacc, nin, nxt_send.at[1], nxt_recv.at[1], at(me, above))
    last_next.start()
    for k in range(CHUNKS):
        for d in range(1, 8):
            z_copy(k, d).wait()
        total = zbuf[k, 0]
        for d in range(1, 8):
            total = total + zbuf[k, d]
        gout[32 * k + 16 * c + index] = total
        each_peer(lambda d: xy_back(k, d).start())
    for k in range(CHUNKS):
        each_peer(lambda d: xy_back(k, d).wait())
        core_back(k).start()
    last_next.wait()
    out[...] += nin[...]
    for k in range(CHUNKS):
        core_back(k).wait()


def fused(offsets, cnt, shard, probe, pat, tab):
    vm = pl.BlockSpec(memory_space=pltpu.VMEM)
    sm = pl.BlockSpec(memory_space=pltpu.SMEM)
    hbm = pl.BlockSpec(memory_space=pltpu.HBM)
    dma = pltpu.SemaphoreType.DMA
    vmem = pltpu.VMEM
    return pl.pallas_call(
        fused_kernel,
        out_shape=[
            jax.ShapeDtypeStruct((32, 1024), f32),
            jax.ShapeDtypeStruct((32 * CHUNKS, UNIT, SIDE), f32),
        ],
        in_specs=[sm, sm, hbm, hbm, hbm, hbm],
        out_specs=[vm, vm],
        scratch_shapes=[
            vmem((1, SIDE), jnp.int32),
            vmem((32, 1024), bf16),
            vmem((MODES, 2, SIDE, SIDE), f32),
            vmem((SLOTS, SIDE, SIDE), f32),
            vmem((10, 256, 256), bf16),
            vmem((32, 1024), bf16),
            vmem((9, 32, SIDE), f32),
            vmem((9, 32, SIDE), f32),
            vmem((SLOTS, PEERS, 32, SIDE), bf16),
            vmem((SLOTS, PEERS, 32, SIDE), bf16),
            vmem((PEERS, 1, SIDE), jnp.int32),
            pltpu.SMEM((PEERS, 1, SIDE), jnp.int32),
            vmem((4, 256, SIDE), f32),
            vmem((4, SIDE, SIDE), f32),
            vmem((MODES, 2, SIDE, SIDE), f32),
            vmem((MODES, 2, SIDE, SIDE), f32),
            vmem((SIDE, SIDE), f32),
            vmem((32 * CHUNKS, UNIT, SIDE), f32),
            vmem((SLOTS, PEERS, 32, SIDE), f32),
            vmem((SLOTS, PEERS, 32, SIDE), f32),
            vmem((32, 1024), f32),
            vmem((32, 1024), f32),
            vmem((CHUNKS, 16, UNIT, SIDE), f32),
            vmem((CHUNKS, 16, UNIT, SIDE), f32),
            vmem((CHUNKS, 16, UNIT, SIDE), f32),
            vmem((CHUNKS, 8, UNIT, SIDE), f32),
            dma((5,)), dma((PEERS,)), dma((PEERS,)), dma((2,)), dma((2,)),
            dma((SLOTS, PEERS)), dma((SLOTS, PEERS)), dma((SLOTS, PEERS)), dma((SLOTS, PEERS)),
            dma((2 * CHUNKS,)), dma((2 * CHUNKS,)), dma((2 * CHUNKS, PEERS)), dma((2 * CHUNKS, PEERS)),
            dma((CHUNKS, 8)), dma((CHUNKS, 8)),
        ],
        compiler_params=pltpu.CompilerParams(
            collective_id=0, has_side_effects=True, vmem_limit_bytes=40 << 20
        ),
        name="ptychography",
    )(pltpu.with_memory_space_constraint(offsets, pltpu.HBM), cnt, *[pltpu.with_memory_space_constraint(v, pltpu.HBM) for v in (shard, probe, pat, tab)])


def per_device(object_slices, probe_modes, offsets, counts, patterns):
    shard = object_slices.reshape(32, 1024)
    out, gout = fused(offsets.reshape(SLOTS, 2).T, counts, shard, probe_modes, patterns[0, 0], jnp.asarray(tables(SIDE)))
    return out.reshape(object_slices.shape), gout.reshape(probe_modes.shape)


def solution(mesh):
    placed = (
        P("tile", None, None, "pos", None),
        P(),
        P("tile", "pos", None, None),
        P("tile", "pos"),
        P("tile", "pos", None, None, None),
    )
    return jax.shard_map(
        per_device,
        mesh=mesh,
        in_specs=placed,
        out_specs=(P("tile", None, None, "pos", None), P()),
        check_vma=False,
    )
```
